256 devices in a mesh: tile: 64 (over z, x, core), occ: 4 (over y).
Axes of the slice: x: 4, y: 4, z: 8, core: 2. Of those that a mesh axis runs over, the one named last changes fastest.
Arguments:
- amplitudes: bfloat16 [8, 512, 128, 128], P('occ', 'tile'), may hold values from -6 to 6
- exchange_ints: bfloat16 [8, 512, 128, 128], P('occ', 'tile'), may hold values from -6 to 6
- left_factors: bfloat16 [1024, 128, 128], P('tile'), may hold values from -0.5 to 0.5
- right_factors: bfloat16 [1024, 128, 128], P('tile'), may hold values from -0.1875 to 0.1875
- ladder_sources: int32 [2048, 8], P('tile'), may hold values from 0 to 7
- ladder_factors: int32 [2048, 8], P('tile'), may hold values from 0 to 15
- dest_owners: int32 [2048, 1], P('tile'), may hold values from 0 to 63; in each aligned block of 32 rows (0 to 31, 32 to 63, ...) at most 2 rows name the same one
- dest_slots: int32 [2048], P('tile'), may hold values from 0 to 7
- cycle_blocks: int32 [512], P('tile'), may hold values from 0 to 1
- cycle_ints: bfloat16 [128, 1024, 1024], P('tile', 'occ'), may hold values from -0.1875 to 0.1875
Outputs:
- residual: bfloat16 [8, 512, 128, 128], P('occ', 'tile')
The draws below stay inside these ranges and needn't reach their ends.
Inputs may be any that keep to these rules, and one draw needn't show every extreme that they name: `dest_owners`: among the rows of one tile index, at most 2 name the same owner, a bound that some block reaches.
All inputs are finite; a program needn't handle non-finite values.
Results may differ from the reference program's by a relative error of at most 0.0053.
Values may be sent and summed in bfloat16 or wider, within the bound.
A program may use at most 128 MiB of HBM per device.

```python
import math
import jax
import jax.numpy as jnp
import numpy as np
from jax import lax

TW = 128
OCC_SLAB = 8
SLOTS_DEV = 8
SLOTS = 512
TERMS_DEV = 32
TERMS = 2048
LAD_K = 8
NFAC_DEV = 16
FACTORS = 1024
CAP = 2
RBLK_DEV = 2
RBLOCKS = 128
N_TILE = 64


def plant(array, stream_key, low, largest):
    longest = array.shape.index(max(array.shape))
    spots = []
    for shift in (0, 1):
        where = [jax.random.randint(jax.random.fold_in(stream_key, axis), (), 0, length) for axis, length in enumerate(array.shape)]
        where[longest] = (where[longest] + shift) % array.shape[longest]
        spots.append(tuple(where))
    return array.at[spots[0]].set(low).at[spots[1]].set(largest)


def levels(key, shape, shards, least, largest):
    def one(dim, blocks):
        heights = jax.random.uniform(jax.random.fold_in(jax.random.fold_in(key, 6), dim), (blocks,), jnp.float32, least / len(shards), largest / len(shards))
        return jnp.repeat(jnp.exp(heights), shape[dim] // blocks).reshape((-1,) + (1,) * (len(shape) - dim - 1))

    gain = one(*shards[0])
    for cut in shards[1:]:
        gain = gain * one(*cut)
    return gain


def shared_out(stream_key, own, number, rows, count, top, limit, slope):
    sequence = jax.random.permutation(stream_key, count)
    crowded, common = shares(count, rows * top, limit, slope, True), shares(count, rows * top, limit, slope, False)
    places = jnp.arange(count)

    def named(tallies, offset_by):
        used = int((tallies > 0).sum())
        fixed = max(1, used // 4)
        moved = fixed + (places - fixed + offset_by * (used - fixed)) % max(1, count - fixed)
        return jnp.zeros((count,), jnp.int32).at[sequence[jnp.where(places < fixed, places, moved)]].set(jnp.asarray(tallies, jnp.int32))

    tallies = jnp.where(number % 4 == 0, named(crowded, number // 4), named(common, number - number // 4 - 1))
    mixed = jax.random.permutation(jax.random.fold_in(own, 3), count)
    giver, sink = mixed[0:count // 2 * 2:2], mixed[1:count // 2 * 2:2]
    room = jnp.minimum(tallies[giver] - 1, limit - tallies[sink]) // 2
    room = jnp.where((giver == sequence[0]) | (sink == sequence[0]) | (tallies[sink] == 0), 0, jnp.maximum(room, 0))
    moved = jax.random.randint(jax.random.fold_in(own, 4), (count // 2,), 0, 1 << 20) % (room + 1)
    tallies = tallies.at[giver].add(-moved).at[sink].add(moved)
    labels = jnp.searchsorted(jnp.cumsum(tallies), jnp.arange(rows * top), side="right").astype(jnp.int32)
    grid = labels.reshape(top, rows).T
    grid = grid[jax.random.permutation(jax.random.fold_in(own, 1), rows)]
    offset_by = jax.random.randint(jax.random.fold_in(own, 2), (rows, 1), 0, top)
    return jnp.take_along_axis(grid, (jnp.arange(top)[None, :] + offset_by) % top, axis=1)


def shares(number_of, total, bound, skew, full):
    portions = [(1 << 20) // math.isqrt(grade ** skew) + 1 for grade in range(1, number_of + 1)]
    largest = bound if full else min(bound, max(-(-total // number_of), total * portions[0] // sum(portions)))
    least = 1 if total - largest >= number_of - 1 else 0
    counts, surplus = [largest] + [least] * (number_of - 1), total - largest - least * (number_of - 1)
    while surplus > 0:
        movable = [i for i in range(1, number_of) if counts[i] < largest] or [i for i in range(1, number_of) if counts[i] < bound]
        pool, budget = sum([portions[i] for i in movable]), surplus
        for i in movable:
            extra = min(bound - counts[i], max(1, budget * portions[i] // pool), surplus)
            counts[i] = counts[i] + extra
            surplus = surplus - extra
    return np.array(counts)


def normal_values(key, extent, scale, reach, shards=(), kind=jnp.bfloat16):
    drawn = scale * jax.random.normal(key, extent, jnp.float32)
    if shards:
        drawn = drawn * levels(key, extent, shards, -0.22, 0.18)
    return jnp.clip(drawn, -reach, reach).astype(kind)


def setup_inputs(seed: int = 0) -> dict:
    key_list = jax.random.split(jax.random.key(seed), 11)
    amplitudes = normal_values(key_list[0], (OCC_SLAB, SLOTS, TW, TW), 1.0, 6.0, ((0, 4), (1, 64)))
    exchange_ints = normal_values(key_list[1], (OCC_SLAB, SLOTS, TW, TW), 1.0, 6.0, ((0, 4), (1, 64)))
    left_factors = normal_values(key_list[2], (FACTORS, TW, TW), TW ** -0.5, 0.5, ((0, 64),))
    right_factors = normal_values(key_list[3], (FACTORS, TW, TW), (TW * LAD_K) ** -0.5, 0.1875, ((0, 64),))
    ladder_sources = plant(jax.random.randint(key_list[4], (TERMS, LAD_K), 0, SLOTS_DEV), jax.random.fold_in(key_list[4], 1), 0, SLOTS_DEV - 1).astype(jnp.int32)
    ladder_factors = plant(jax.random.randint(key_list[5], (TERMS, LAD_K), 0, NFAC_DEV), jax.random.fold_in(key_list[5], 1), 0, NFAC_DEV - 1).astype(jnp.int32)
    dest_owners_keys = jax.random.split(jax.random.fold_in(key_list[6], 1), TERMS // TERMS_DEV)
    dest_owners_turns = jax.random.permutation(jax.random.fold_in(key_list[6], 3), TERMS // TERMS_DEV)
    dest_owners = jax.vmap(lambda own, number: shared_out(jax.random.fold_in(key_list[6], 2), own, number, TERMS_DEV, N_TILE, 1, CAP, 2))(dest_owners_keys, dest_owners_turns).reshape((TERMS, 1))
    dest_slots = plant(jax.random.randint(key_list[7], (TERMS,), 0, SLOTS_DEV), jax.random.fold_in(key_list[7], 1), 0, SLOTS_DEV - 1).astype(jnp.int32)
    cycle_blocks = plant(jax.random.randint(key_list[8], (SLOTS,), 0, RBLK_DEV), jax.random.fold_in(key_list[8], 1), 0, RBLK_DEV - 1).astype(jnp.int32)
    cycle_ints = normal_values(key_list[9], (RBLOCKS, OCC_SLAB * TW, OCC_SLAB * TW), (OCC_SLAB * TW) ** -0.5, 0.1875, ((0, 64), (1, 4)))
    return {"amplitudes": amplitudes, "exchange_ints": exchange_ints, "left_factors": left_factors, "right_factors": right_factors, "ladder_sources": ladder_sources, "ladder_factors": ladder_factors, "dest_owners": dest_owners, "dest_slots": dest_slots, "cycle_blocks": cycle_blocks, "cycle_ints": cycle_ints}


def owner_terms(owner_block, amplitudes, left_factors, right_factors, ladder_sources, ladder_factors):
    sources = lax.dynamic_slice_in_dim(ladder_sources, owner_block * TERMS_DEV, TERMS_DEV, 0) + owner_block * SLOTS_DEV
    factor_ids = lax.dynamic_slice_in_dim(ladder_factors, owner_block * TERMS_DEV, TERMS_DEV, 0) + owner_block * NFAC_DEV
    running = jnp.zeros((OCC_SLAB, TERMS_DEV, TW, TW), jnp.float32)
    for factor_index in range(LAD_K):
        left_tiles = jnp.take(left_factors, factor_ids[:, factor_index], axis=0).astype(jnp.float32)
        amp_tiles = jnp.take(amplitudes, sources[:, factor_index], axis=1).astype(jnp.float32)
        half_prod = jnp.einsum('gac,jgcd->jgad', left_tiles, amp_tiles)
        half_prod = lax.optimization_barrier(half_prod.astype(jnp.bfloat16)).astype(jnp.float32)
        right_tiles = jnp.take(right_factors, factor_ids[:, factor_index], axis=0).astype(jnp.float32)
        running = running + jnp.einsum('jgad,gbd->jgab', half_prod, right_tiles)
    return running.astype(jnp.bfloat16)


def reference(amplitudes, exchange_ints, left_factors, right_factors, ladder_sources, ladder_factors, dest_owners, dest_slots, cycle_blocks, cycle_ints):
    def ladder_step(owner_block, carry):
        partial_value = owner_terms(owner_block, amplitudes, left_factors, right_factors, ladder_sources, ladder_factors)
        owners_here = lax.dynamic_slice_in_dim(dest_owners[:, 0], owner_block * TERMS_DEV, TERMS_DEV, 0)
        slots_here = lax.dynamic_slice_in_dim(dest_slots, owner_block * TERMS_DEV, TERMS_DEV, 0)
        targets = owners_here * SLOTS_DEV + slots_here
        return carry.at[:, targets].add(partial_value.astype(jnp.float32))

    ladder = lax.fori_loop(0, N_TILE, ladder_step, jnp.zeros((OCC_SLAB, SLOTS, TW, TW), jnp.float32))

    def cycle_owner(owner_block):
        amp_tiles = lax.dynamic_slice_in_dim(amplitudes, owner_block * SLOTS_DEV, SLOTS_DEV, 1).astype(jnp.float32)
        block_ids = lax.dynamic_slice_in_dim(cycle_blocks, owner_block * SLOTS_DEV, SLOTS_DEV, 0) + owner_block * RBLK_DEV
        cycle_mats = jnp.take(cycle_ints, block_ids, axis=0).astype(jnp.float32)
        amp_matrix = amp_tiles.transpose(1, 2, 0, 3).reshape(SLOTS_DEV, TW, OCC_SLAB * TW)
        product = jnp.einsum('sak,skn->san', amp_matrix, cycle_mats)
        return product.reshape(SLOTS_DEV, TW, OCC_SLAB, TW).transpose(2, 0, 1, 3)

    cycle_part = lax.map(cycle_owner, jnp.arange(N_TILE, dtype=jnp.int32))
    cycle_part = cycle_part.transpose(1, 0, 2, 3, 4).reshape(OCC_SLAB, SLOTS, TW, TW)
    return (exchange_ints.astype(jnp.float32) + ladder + cycle_part).astype(jnp.bfloat16)
```

```python
import functools

import jax
import jax.numpy as jnp
from jax import lax
from jax.experimental import pallas as pl
from jax.experimental.pallas import tpu as pltpu
from jax.sharding import PartitionSpec as P

MESH = pl.DeviceIdType.MESH
NZ, NX, NC = 8, 4, 2
TERMS = 32
SLOTS = 8
TW = 128
J = 2
ROWS = 32
PARTS = TW // ROWS
CHUNKS = J * PARTS
RING = 5
SMALL_CAP, SMALL_ENTRIES = 14, 80


def cycle_kernel(blocks_ref, amp_ref, ints_ref, out_ref):
    def one(s, _):
        ints = ints_ref.at[blocks_ref[s]]
        rows = jnp.concatenate([amp_ref[0, s], amp_ref[1, s]], axis=1)
        prod = jnp.dot(rows, ints[...], preferred_element_type=jnp.float32)
        for j in range(8):
            out_ref[j, s] = prod[:, j * TW : (j + 1) * TW].astype(jnp.bfloat16)
        return 0

    lax.fori_loop(0, SLOTS, one, 0)


def cycle_products(cycle_blocks, amplitudes, cycle_ints):
    vmem = pl.BlockSpec(memory_space=pltpu.VMEM)
    return pl.pallas_call(
        cycle_kernel,
        out_shape=jax.ShapeDtypeStruct((8, SLOTS, TW, TW), jnp.bfloat16),
        in_specs=[pl.BlockSpec(memory_space=pltpu.SMEM), vmem, vmem],
        out_specs=vmem,
        compiler_params=pltpu.CompilerParams(vmem_limit_bytes=32 * 2**20),
        cost_estimate=pl.CostEstimate(
            flops=2 * SLOTS * TW * 256 * 1024, bytes_accessed=4 * 2**20, transcendentals=0
        ),
    )(cycle_blocks, amplitudes, cycle_ints)


def ladder_kernel(src_ref, fac_ref, pos_ref, amp_ref, left_ref, right_ref, out_ref, rt, stage, sem):
    for f in range(16):
        rt[f] = right_ref[f].T

    def put(g):
        return pltpu.make_async_copy(stage.at[g], out_ref.at[:, pos_ref[g]], sem.at[g])

    def one(g, _):
        acc = jnp.zeros((2 * TW, TW), jnp.float32)
        for q in range(8):
            s = src_ref[g, q]
            f = fac_ref[g, q]
            amps = jnp.concatenate([amp_ref[0, s], amp_ref[1, s]], axis=1)
            half = jnp.dot(left_ref[f], amps, preferred_element_type=jnp.float32).astype(
                jnp.bfloat16
            )
            both = jnp.concatenate([half[:, :TW], half[:, TW:]], axis=0)
            acc = acc + jnp.dot(both, rt[f], preferred_element_type=jnp.float32)
        stage[g] = acc.astype(jnp.bfloat16).reshape(J, TW, TW)
        put(g).start()
        return 0

    lax.fori_loop(0, TERMS, one, 0)

    def finish(g, _):
        put(g).wait()
        return 0

    lax.fori_loop(0, TERMS, finish, 0)


def ladder_terms(sources, factors, places, amplitudes, left, right):
    smem = pl.BlockSpec(memory_space=pltpu.SMEM)
    vmem = pl.BlockSpec(memory_space=pltpu.VMEM)
    return pl.pallas_call(
        ladder_kernel,
        out_shape=jax.ShapeDtypeStruct((J, NX * TERMS, TW, TW), jnp.bfloat16),
        in_specs=[smem, smem, smem, vmem, vmem, vmem],
        out_specs=pl.BlockSpec(memory_space=pl.ANY),
        scratch_shapes=[
            pltpu.VMEM((16, TW, TW), jnp.bfloat16),
            pltpu.VMEM((TERMS, J, TW, TW), jnp.bfloat16),
            pltpu.SemaphoreType.DMA((TERMS,)),
        ],
        compiler_params=pltpu.CompilerParams(vmem_limit_bytes=32 * 2**20),
        cost_estimate=pl.CostEstimate(
            flops=2 * 1024 * TW**3, bytes_accessed=4 * 2**20, transcendentals=0
        ),
    )(sources, factors, places, amplitudes, left, right)


def route_kernel(
    cap, entries, perm_ref, same_ref, end_ref, some_ref, p_ref, out_ref,
    recv, stage, sums, zs, zr, xs_sem, fs_sem, lx_sem, rx_sem, zs_sem, zr_sem,
):
    t = lax.axis_index("tile")
    y = lax.axis_index("occ")
    core = t % NC
    x = (t // NC) % NX
    z = t // (NC * NX)
    m = t % (NC * NX)

    def at(zz, xx, cc):
        return {"tile": (zz * NX + xx) * NC + cc, "occ": y}

    sibling = at(z, x, 1 - core)
    ups = at((z + 1) % NZ, x, core)
    downs = at((z + NZ - 1) % NZ, x, core)
    barrier = pltpu.get_barrier_semaphore()
    partners = [at(z, (x + d) % NX, core) for d in range(1, NX)] + [sibling, ups, downs]
    for partner in partners:
        pl.semaphore_signal(barrier, inc=1, device_id=partner, device_id_type=MESH)
    pl.semaphore_wait(barrier, len(partners))

    def mine(h, xx):
        return p_ref.at[h // PARTS, xx, pl.ds(0, cap), pl.ds((h % PARTS) * ROWS, ROWS)]

    def send_x(h, d):
        xx = (x + d) % NX
        return pltpu.make_async_remote_copy(
            src_ref=mine(h, xx), dst_ref=recv.at[h, m],
            send_sem=xs_sem.at[h, d], recv_sem=rx_sem.at[h, m],
            device_id=at(z, xx, core), device_id_type=MESH,
        )

    def send_own(h):
        return pltpu.make_async_remote_copy(
            src_ref=mine(h, x), dst_ref=recv.at[h, m],
            send_sem=xs_sem.at[h, 0], recv_sem=rx_sem.at[h, m],
            device_id=sibling, device_id_type=MESH,
        )

    def copy_own(h):
        return pltpu.make_async_copy(mine(h, x), recv.at[h, m], lx_sem.at[h])

    def forward(h, d):
        source = ((x + d) % NX) * NC + core
        return pltpu.make_async_remote_copy(
            src_ref=recv.at[h, source], dst_ref=recv.at[h, source],
            send_sem=fs_sem.at[h, d], recv_sem=rx_sem.at[h, source],
            device_id=sibling, device_id_type=MESH,
        )

    def arrived(h, source):
        return pltpu.make_async_copy(recv.at[h, source], recv.at[h, source], rx_sem.at[h, source])

    def start_x(h):
        for d in range(1, NX):
            send_x(h, d).start()
        send_own(h).start()
        copy_own(h).start()

    def send_z(h, way, step):
        if step == 0:
            part = pl.ds(4 * way, 4)
        else:
            part = pl.ds(0, SLOTS)
        return pltpu.make_async_remote_copy(
            src_ref=zs.at[h, way, step, part], dst_ref=zr.at[h, way, step, part],
            send_sem=zs_sem.at[h, way, step], recv_sem=zr_sem.at[h, way, step],
            device_id=ups if way == 0 else downs, device_id_type=MESH,
        )

    def own(h, zz, s):
        place = zz * SLOTS + s
        value = sums[h % RING, end_ref[place]]
        return jnp.where(some_ref[place] != 0, value, 0.0)

    def z_step(h, step):
        for way in range(2):
            if step > 0:
                send_z(h, way, step - 1).wait_recv()
            zz = (z + 4 - step) % NZ if way == 0 else (z + 4 + step) % NZ
            for s in range(4 * way, 4 * way + 4) if step == 0 else range(SLOTS):
                value = own(h, zz, s)
                if step > 1 or (step == 1 and s // 4 == way):
                    value = value + zr[h, way, step - 1, s].astype(jnp.float32)
                zs[h, way, step, s] = value.astype(jnp.bfloat16)
            send_z(h, way, step).start()

    def finish(h):
        for way in range(2):
            send_z(h, way, 3).wait_recv()
        for s in range(SLOTS):
            total = own(h, z, s) + zr[h, 0, 3, s].astype(jnp.float32)
            total = total + zr[h, 1, 3, s].astype(jnp.float32)
            out_ref[h // PARTS, s, pl.ds((h % PARTS) * ROWS, ROWS)] = total

    def collect(h):
        for d in range(1, NX):
            arrived(h, ((x + d) % NX) * NC + core).wait()
            forward(h, d).start()
        copy_own(h).wait()
        for d in range(NX):
            arrived(h, ((x + d) % NX) * NC + 1 - core).wait()
        for source in range(NX * NC):
            stage[source * cap : (source + 1) * cap] = recv[h, source]

        def entry(e, total):
            value = stage[perm_ref[e]].astype(jnp.float32)
            total = value + jnp.where(same_ref[e] != 0, total, 0.0)
            sums[h % RING, e] = total
            return total

        lax.fori_loop(0, entries, entry, jnp.zeros((ROWS, TW), jnp.float32), unroll=4)

    start_x(0)

    def turn(i, _):
        @pl.when(i + 1 < CHUNKS)
        def _():
            start_x(i + 1)

        @pl.when(i < CHUNKS)
        def _():
            collect(i)
            z_step(i, 0)

        for step in range(1, 4):
            @pl.when((i >= step) & (i - step < CHUNKS))
            def _(step=step):
                z_step(i - step, step)

        @pl.when(i >= 4)
        def _():
            finish(i - 4)

        return 0

    lax.fori_loop(0, CHUNKS + 4, turn, 0)

    def drain(h, _):
        for d in range(1, NX):
            send_x(h, d).wait_send()
            forward(h, d).wait_send()
        send_own(h).wait_send()
        for way in range(2):
            for step in range(4):
                send_z(h, way, step).wait_send()
        return 0

    lax.fori_loop(0, CHUNKS, drain, 0)


def route(cap, entries, collective_id, perm, same, end, some, packed):
    smem = pl.BlockSpec(memory_space=pltpu.SMEM)
    dma = pltpu.SemaphoreType.DMA
    return pl.pallas_call(
        functools.partial(route_kernel, cap, entries),
        out_shape=jax.ShapeDtypeStruct((J, SLOTS, TW, TW), jnp.float32),
        in_specs=[smem, smem, smem, smem, pl.BlockSpec(memory_space=pl.ANY)],
        out_specs=pl.BlockSpec(memory_space=pltpu.VMEM),
        scratch_shapes=[
            pltpu.VMEM((CHUNKS, NX * NC, cap, ROWS, TW), jnp.bfloat16),
            pltpu.VMEM((NX * NC * cap, ROWS, TW), jnp.bfloat16),
            pltpu.VMEM((RING, entries, ROWS, TW), jnp.float32),
            pltpu.VMEM((CHUNKS, 2, 4, SLOTS, ROWS, TW), jnp.bfloat16),
            pltpu.VMEM((CHUNKS, 2, 4, SLOTS, ROWS, TW), jnp.bfloat16),
            dma((CHUNKS, NX)),
            dma((CHUNKS, NX)),
            dma((CHUNKS,)),
            dma((CHUNKS, NX * NC)),
            dma((CHUNKS, 2, 4)),
            dma((CHUNKS, 2, 4)),
        ],
        compiler_params=pltpu.CompilerParams(
            collective_id=collective_id, has_side_effects=True, vmem_limit_bytes=56 * 2**20
        ),
        cost_estimate=pl.CostEstimate(
            flops=2**22, bytes_accessed=8 * 2**20, transcendentals=0
        ),
    )(perm, same, end, some, packed)


def ranks_in_column(keys):
    column = (keys // (SLOTS * NC)) % NX
    order = jnp.arange(TERMS, dtype=jnp.int32)
    earlier = order[:, None] > order[None, :]
    alike = column[..., :, None] == column[..., None, :]
    return column, jnp.sum((alike & earlier).astype(jnp.int32), axis=-1)


def local(
    amplitudes, exchange_ints, left_factors, right_factors, ladder_sources, ladder_factors,
    dest_owners, dest_slots, cycle_blocks, cycle_ints,
):
    tile = lax.axis_index("tile")
    keys = dest_owners[:, 0] * SLOTS + dest_slots
    table = lax.all_gather(keys, "tile", axis=0)

    product = cycle_products(cycle_blocks, amplitudes, cycle_ints)
    cycle_part = lax.psum_scatter(product, "occ", scatter_dimension=0, tiled=True)

    column, rank = ranks_in_column(keys)
    packed = ladder_terms(
        ladder_sources, ladder_factors, column * TERMS + rank, amplitudes, left_factors,
        right_factors,
    ).reshape(J, NX, TERMS, TW, TW)

    all_ranks = ranks_in_column(table)[1]
    owner = table // SLOTS
    crowd = jnp.sum(
        (owner.reshape(NZ, 8 * TERMS)[:, :, None] % 8 == jnp.arange(8)).astype(jnp.int32), axis=1
    )
    fits = (jnp.max(all_ranks) < SMALL_CAP) & (jnp.max(crowd) <= SMALL_ENTRIES)

    group = (tile // 8) * 8
    here = lax.dynamic_slice_in_dim(table, group, 8, 0).reshape(-1)
    here_rank = lax.dynamic_slice_in_dim(all_ranks, group, 8, 0).reshape(-1)
    number = jnp.arange(8 * TERMS, dtype=jnp.int32)
    valid = (here // SLOTS) % 8 == tile % 8
    target = jnp.where(valid, (here // (SLOTS * 8)) * SLOTS + here % SLOTS, 64)
    order = target * 256 + number
    place = jnp.sum((order[None, :] < order[:, None]).astype(jnp.int32), axis=1)
    hit = place[None, :] == number[:, None]
    source = number // TERMS
    perm_small = jnp.sum(jnp.where(hit, source * SMALL_CAP + here_rank, 0), axis=1)
    perm_full = jnp.sum(jnp.where(hit, source * TERMS + here_rank, 0), axis=1)
    sorted_target = jnp.sum(jnp.where(hit, target, 0), axis=1)
    same = jnp.concatenate(
        [jnp.zeros((1,), jnp.int32), (sorted_target[1:] == sorted_target[:-1]).astype(jnp.int32)]
    )
    goal = jnp.arange(64, dtype=jnp.int32)[:, None]
    end = jnp.maximum(jnp.sum((target[None, :] <= goal).astype(jnp.int32), axis=1) - 1, 0)
    some = jnp.sum((target[None, :] == goal).astype(jnp.int32), axis=1)

    def small():
        return route(
            SMALL_CAP, SMALL_ENTRIES, 0, perm_small[:SMALL_ENTRIES], same[:SMALL_ENTRIES],
            end, some, packed,
        )

    def full():
        return route(TERMS, 8 * TERMS, 1, perm_full, same, end, some, packed)

    ladder = lax.cond(fits, small, full)
    return (
        exchange_ints.astype(jnp.float32) + ladder + cycle_part.astype(jnp.float32)
    ).astype(jnp.bfloat16)


def solution(mesh):
    placed = (
        P("occ", "tile", None, None),
        P("occ", "tile", None, None),
        P("tile", None, None),
        P("tile", None, None),
        P("tile", None),
        P("tile", None),
        P("tile", None),
        P("tile"),
        P("tile"),
        P("tile", "occ", None),
    )
    return jax.shard_map(
        local, mesh=mesh, in_specs=placed, out_specs=P("occ", "tile", None, None), check_vma=False
    )
```

```python
import functools

import jax
import jax.numpy as jnp
from jax import lax
from jax.experimental import pallas as pl
from jax.experimental.pallas import tpu as pltpu
from jax.sharding import PartitionSpec as P

MESH = pl.DeviceIdType.MESH
NZ, NX, NC = 8, 4, 2
TERMS = 32
SLOTS = 8
TW = 128
J = 2
ROWS = 32
PARTS = TW // ROWS
CHUNKS = J * PARTS
RING = 5
CAP = 14
LANES = 128


def ladder_kernel(src_ref, fac_ref, pos_ref, amp_ref, left_ref, right_ref, out_ref, rt, stage, sem):
    for f in range(16):
        rt[f] = right_ref[f].T

    def put(g):
        return pltpu.make_async_copy(stage.at[g], out_ref.at[:, pos_ref[g]], sem.at[g])

    def one(g, _):
        acc = jnp.zeros((2 * TW, TW), jnp.float32)
        for q in range(8):
            s = src_ref[g, q]
            f = fac_ref[g, q]
            amps = jnp.concatenate([amp_ref[0, s], amp_ref[1, s]], axis=1)
            half = jnp.dot(left_ref[f], amps, preferred_element_type=jnp.float32).astype(
                jnp.bfloat16
            )
            both = jnp.concatenate([half[:, :TW], half[:, TW:]], axis=0)
            acc = acc + jnp.dot(both, rt[f], preferred_element_type=jnp.float32)
        stage[g] = acc.astype(jnp.bfloat16).reshape(J, TW, TW)
        put(g).start()
        return 0

    lax.fori_loop(0, TERMS, one, 0)

    def finish(g, _):
        put(g).wait()
        return 0

    lax.fori_loop(0, TERMS, finish, 0)


def ladder_terms(sources, factors, places, amplitudes, left, right):
    smem = pl.BlockSpec(memory_space=pltpu.SMEM)
    vmem = pl.BlockSpec(memory_space=pltpu.VMEM)
    return pl.pallas_call(
        ladder_kernel,
        out_shape=jax.ShapeDtypeStruct((J, NX * TERMS, TW, TW), jnp.bfloat16),
        in_specs=[smem, smem, smem, vmem, vmem, vmem],
        out_specs=pl.BlockSpec(memory_space=pl.ANY),
        scratch_shapes=[
            pltpu.VMEM((16, TW, TW), jnp.bfloat16),
            pltpu.VMEM((TERMS, J, TW, TW), jnp.bfloat16),
            pltpu.SemaphoreType.DMA((TERMS,)),
        ],
        compiler_params=pltpu.CompilerParams(vmem_limit_bytes=32 * 2**20),
        cost_estimate=pl.CostEstimate(
            flops=2 * 1024 * TW**3, bytes_accessed=4 * 2**20, transcendentals=0
        ),
    )(sources, factors, places, amplitudes, left, right)


def route_kernel(
    first, cap, entries, perm_ref, same_ref, end_ref, some_ref, p_ref, out_ref,
    recv, stage, sums, zs, zr, xs_sem, fs_sem, lx_sem, rx_sem, zs_sem, zr_sem,
):
    t = lax.axis_index("tile")
    y = lax.axis_index("occ")
    core = t % NC
    x = (t // NC) % NX
    z = t // (NC * NX)
    m = t % (NC * NX)

    def at(zz, xx, cc):
        return {"tile": (zz * NX + xx) * NC + cc, "occ": y}

    sibling = at(z, x, 1 - core)
    ups = at((z + 1) % NZ, x, core)
    downs = at((z + NZ - 1) % NZ, x, core)
    barrier = pltpu.get_barrier_semaphore()
    partners = [at(z, (x + d) % NX, core) for d in range(1, NX)] + [sibling, ups, downs]
    for partner in partners:
        pl.semaphore_signal(barrier, inc=1, device_id=partner, device_id_type=MESH)
    pl.semaphore_wait(barrier, len(partners))

    def mine(h, xx):
        return p_ref.at[h // PARTS, xx, pl.ds(first, cap), pl.ds((h % PARTS) * ROWS, ROWS)]

    def send_x(h, d):
        xx = (x + d) % NX
        return pltpu.make_async_remote_copy(
            src_ref=mine(h, xx), dst_ref=recv.at[h, m],
            send_sem=xs_sem.at[h, d], recv_sem=rx_sem.at[h, m],
            device_id=at(z, xx, core), device_id_type=MESH,
        )

    def send_own(h):
        return pltpu.make_async_remote_copy(
            src_ref=mine(h, x), dst_ref=recv.at[h, m],
            send_sem=xs_sem.at[h, 0], recv_sem=rx_sem.at[h, m],
            device_id=sibling, device_id_type=MESH,
        )

    def copy_own(h):
        return pltpu.make_async_copy(mine(h, x), recv.at[h, m], lx_sem.at[h])

    def forward(h, d):
        source = ((x + d) % NX) * NC + core
        return pltpu.make_async_remote_copy(
            src_ref=recv.at[h, source], dst_ref=recv.at[h, source],
            send_sem=fs_sem.at[h, d], recv_sem=rx_sem.at[h, source],
            device_id=sibling, device_id_type=MESH,
        )

    def arrived(h, source):
        return pltpu.make_async_copy(recv.at[h, source], recv.at[h, source], rx_sem.at[h, source])

    def start_x(h):
        for d in range(1, NX):
            send_x(h, d).start()
        send_own(h).start()
        copy_own(h).start()

    def send_z(h, way, step):
        if step == 0:
            part = pl.ds(4 * way, 4)
        else:
            part = pl.ds(0, SLOTS)
        return pltpu.make_async_remote_copy(
            src_ref=zs.at[h, way, step, part], dst_ref=zr.at[h, way, step, part],
            send_sem=zs_sem.at[h, way, step], recv_sem=zr_sem.at[h, way, step],
            device_id=ups if way == 0 else downs, device_id_type=MESH,
        )

    def own(h, zz, s):
        place = zz * SLOTS + s
        value = sums[h % RING, end_ref[place]]
        return jnp.where(some_ref[place] != 0, value, 0.0)

    def z_step(h, step):
        for way in range(2):
            if step > 0:
                send_z(h, way, step - 1).wait_recv()
            zz = (z + 4 - step) % NZ if way == 0 else (z + 4 + step) % NZ
            for s in range(4 * way, 4 * way + 4) if step == 0 else range(SLOTS):
                value = own(h, zz, s)
                if step > 1 or (step == 1 and s // 4 == way):
                    value = value + zr[h, way, step - 1, s].astype(jnp.float32)
                zs[h, way, step, s] = value.astype(jnp.bfloat16)
            send_z(h, way, step).start()

    def finish(h):
        for way in range(2):
            send_z(h, way, 3).wait_recv()
        for s in range(SLOTS):
            total = own(h, z, s) + zr[h, 0, 3, s].astype(jnp.float32)
            total = total + zr[h, 1, 3, s].astype(jnp.float32)
            out_ref[h // PARTS, s, pl.ds((h % PARTS) * ROWS, ROWS)] = total

    def collect(h):
        for d in range(1, NX):
            arrived(h, ((x + d) % NX) * NC + core).wait()
            forward(h, d).start()
        copy_own(h).wait()
        for d in range(NX):
            arrived(h, ((x + d) % NX) * NC + 1 - core).wait()
        for source in range(NX * NC):
            stage[source * cap : (source + 1) * cap] = recv[h, source]

        def entry(e, total):
            value = stage[perm_ref[e]].astype(jnp.float32)
            total = value + jnp.where(same_ref[e] != 0, total, 0.0)
            sums[h % RING, e] = total
            return total

        lax.fori_loop(0, entries, entry, jnp.zeros((ROWS, TW), jnp.float32), unroll=4)

    start_x(0)

    def turn(i, _):
        @pl.when(i + 1 < CHUNKS)
        def _():
            start_x(i + 1)

        @pl.when(i < CHUNKS)
        def _():
            collect(i)
            z_step(i, 0)

        for step in range(1, 4):
            @pl.when((i >= step) & (i - step < CHUNKS))
            def _(step=step):
                z_step(i - step, step)

        @pl.when(i >= 4)
        def _():
            finish(i - 4)

        return 0

    lax.fori_loop(0, CHUNKS + 4, turn, 0)

    def drain(h, _):
        for d in range(1, NX):
            send_x(h, d).wait_send()
            forward(h, d).wait_send()
        send_own(h).wait_send()
        for way in range(2):
            for step in range(4):
                send_z(h, way, step).wait_send()
        return 0

    lax.fori_loop(0, CHUNKS, drain, 0)


def route(first, cap, entries, collective_id, perm, same, end, some, packed):
    smem = pl.BlockSpec(memory_space=pltpu.SMEM)
    dma = pltpu.SemaphoreType.DMA
    return pl.pallas_call(
        functools.partial(route_kernel, first, cap, entries),
        out_shape=jax.ShapeDtypeStruct((J, SLOTS, TW, TW), jnp.float32),
        in_specs=[smem, smem, smem, smem, pl.BlockSpec(memory_space=pl.ANY)],
        out_specs=pl.BlockSpec(memory_space=pltpu.VMEM),
        scratch_shapes=[
            pltpu.VMEM((CHUNKS, NX * NC, cap, ROWS, TW), jnp.bfloat16),
            pltpu.VMEM((NX * NC * cap, ROWS, TW), jnp.bfloat16),
            pltpu.VMEM((RING, entries, ROWS, TW), jnp.float32),
            pltpu.VMEM((CHUNKS, 2, 4, SLOTS, ROWS, TW), jnp.bfloat16),
            pltpu.VMEM((CHUNKS, 2, 4, SLOTS, ROWS, TW), jnp.bfloat16),
            dma((CHUNKS, NX)),
            dma((CHUNKS, NX)),
            dma((CHUNKS,)),
            dma((CHUNKS, NX * NC)),
            dma((CHUNKS, 2, 4)),
            dma((CHUNKS, 2, 4)),
        ],
        compiler_params=pltpu.CompilerParams(
            collective_id=collective_id, has_side_effects=True, vmem_limit_bytes=56 * 2**20
        ),
        cost_estimate=pl.CostEstimate(
            flops=2**22, bytes_accessed=8 * 2**20, transcendentals=0
        ),
    )(perm, same, end, some, packed)


def ranks_in_column(keys):
    column = (keys // (SLOTS * NC)) % NX
    order = jnp.arange(TERMS, dtype=jnp.int32)
    earlier = order[:, None] > order[None, :]
    alike = column[..., :, None] == column[..., None, :]
    return column, jnp.sum((alike & earlier).astype(jnp.int32), axis=-1)


def row_iota(shape, axis):
    return lax.broadcasted_iota(jnp.int32, shape, axis)


def as_column(row):
    diagonal = row_iota((LANES, LANES), 0) == row_iota((LANES, LANES), 1)
    return jnp.sum(jnp.where(diagonal, row, 0), axis=1, keepdims=True)


def main_kernel(
    src_ref, fac_ref, blocks_ref, keys_ref, amp_hbm, exch_hbm, left_hbm, right_hbm, ints_hbm,
    out_ref, flag_ref,
    amp_ref, exch_ref, left_ref, right_ref, ints_ref, rt, terms, packed, recv, stage, sums,
    zs, zr, ysend, yrecv, labels_out, labels_in, flags_out, flags_in, pack_v, plan_v,
    pack_s, plan_s,
    in_sem, xs_sem, fs_sem, lx_sem, rx_sem, zs_sem, zr_sem, ys_sem, yr_sem, ls_sem, lr_sem,
    gs_sem, gr_sem, sm_sem,
):
    t = lax.axis_index("tile")
    y = lax.axis_index("occ")
    core = t % NC
    x = (t // NC) % NX
    z = t // (NC * NX)
    m = t % (NC * NX)

    def at(zz, xx, cc):
        return {"tile": (zz * NX + xx) * NC + cc, "occ": y}

    def at_y(d):
        return {"tile": t, "occ": (y + d) % 4}

    def at_m(d):
        return {"tile": z * (NX * NC) + (m + d) % (NX * NC), "occ": y}

    def at_z(d):
        return at((z + d) % NZ, x, core)

    sibling = at(z, x, 1 - core)
    ups = at_z(1)
    downs = at_z(NZ - 1)

    loads = [
        pltpu.make_async_copy(hbm, ref, in_sem.at[n])
        for n, (hbm, ref) in enumerate(
            [(right_hbm, right_ref), (left_hbm, left_ref), (amp_hbm, amp_ref),
             (ints_hbm, ints_ref), (exch_hbm, exch_ref)]
        )
    ]
    for load in loads:
        load.start()

    barrier = pltpu.get_barrier_semaphore()
    partners = [at_m(d) for d in range(1, NX * NC)] + [at_z(d) for d in range(1, NZ)]
    partners = partners + [at_y(d) for d in range(1, 4)]
    for partner in partners:
        pl.semaphore_signal(barrier, inc=1, device_id=partner, device_id_type=MESH)

    lane = row_iota((LANES, LANES), 1)
    line = row_iota((LANES, LANES), 0)
    keys = keys_ref[...]
    key_column = as_column(keys)
    real = line < TERMS
    column_row = jnp.where(row_iota((1, LANES), 1) < TERMS, (keys // 16) % NX, NX)
    column = (key_column // 16) % NX
    rank = jnp.sum(
        jnp.where((column_row == column) & (lane < line), 1, 0), axis=1, keepdims=True
    )
    pack_v[...] = jnp.broadcast_to(
        jnp.sum(jnp.where(real & (column * TERMS + rank == lane), line, 0), axis=0, keepdims=True),
        (8, LANES),
    )
    label = ((key_column // 8) % NC) * 64 + (key_column // 64) * SLOTS + key_column % SLOTS
    for xx in range(NX):
        here = real & (column == xx) & (rank < CAP) & (m * 16 + rank == lane)
        row = jnp.sum(jnp.where(here, label + 1, 0), axis=0, keepdims=True)
        labels_out[xx] = jnp.broadcast_to(row, (8, LANES))
    over = jnp.max(jnp.where(real & (rank >= CAP), 1, 0), axis=0, keepdims=True)
    labels_out[NX] = jnp.broadcast_to(over, (8, LANES))
    pack_copy = pltpu.make_async_copy(pack_v, pack_s, sm_sem.at[0])
    pack_copy.start()

    pl.semaphore_wait(barrier, len(partners))

    def send_label(d, which):
        if which == 0:
            part = (((m + d) % (NX * NC)) // NC)
        else:
            part = NX
        return pltpu.make_async_remote_copy(
            src_ref=labels_out.at[part], dst_ref=labels_in.at[which, m],
            send_sem=ls_sem.at[which, d], recv_sem=lr_sem.at[which, m],
            device_id=at_m(d), device_id_type=MESH,
        )

    def label_from(d, which):
        source = (m + d) % (NX * NC)
        return pltpu.make_async_copy(
            labels_in.at[which, source], labels_in.at[which, source], lr_sem.at[which, source]
        )

    for d in range(1, NX * NC):
        for which in range(2):
            send_label(d, which).start()
    labels_in[0, m] = labels_out[x]
    labels_in[1, m] = labels_out[NX]

    loads[0].wait()
    for f in range(16):
        rt[f] = right_ref[f].T
    loads[1].wait()
    loads[2].wait()

    def one(g, _):
        halves, rights = [], []
        for q in range(8):
            s = src_ref[g, q]
            f = fac_ref[g, q]
            amps = jnp.concatenate([amp_ref[0, s], amp_ref[1, s]], axis=1)
            half = jnp.dot(left_ref[f], amps, preferred_element_type=jnp.float32).astype(
                jnp.bfloat16
            )
            halves.append(jnp.concatenate([half[:, :TW], half[:, TW:]], axis=0))
            rights.append(rt[f])
        acc = jnp.dot(
            jnp.concatenate(halves, axis=1), jnp.concatenate(rights, axis=0),
            preferred_element_type=jnp.float32,
        )
        terms[g] = acc.astype(jnp.bfloat16).reshape(J, TW, TW)
        return 0

    lax.fori_loop(0, TERMS, one, 0, unroll=4)

    def send_x(h, d):
        xx = (x + d) % NX
        return pltpu.make_async_remote_copy(
            src_ref=packed.at[h, xx], dst_ref=recv.at[h, m],
            send_sem=xs_sem.at[h, d], recv_sem=rx_sem.at[h, m],
            device_id=at(z, xx, core), device_id_type=MESH,
        )

    def send_own(h):
        return pltpu.make_async_remote_copy(
            src_ref=packed.at[h, x], dst_ref=recv.at[h, m],
            send_sem=xs_sem.at[h, 0], recv_sem=rx_sem.at[h, m],
            device_id=sibling, device_id_type=MESH,
        )

    def copy_own(h):
        return pltpu.make_async_copy(packed.at[h, x], recv.at[h, m], lx_sem.at[h])

    def forward(h, d):
        source = ((x + d) % NX) * NC + core
        return pltpu.make_async_remote_copy(
            src_ref=recv.at[h, source], dst_ref=recv.at[h, source],
            send_sem=fs_sem.at[h, d], recv_sem=rx_sem.at[h, source],
            device_id=sibling, device_id_type=MESH,
        )

    def arrived(h, source):
        return pltpu.make_async_copy(recv.at[h, source], recv.at[h, source], rx_sem.at[h, source])

    def start_x(h):
        rows = pl.ds((h % PARTS) * ROWS, ROWS)
        for d in (2, 1, 3, 0):
            xx = (x + d) % NX
            for k in range(CAP):
                packed[h, xx, k] = terms[pack_s[0, xx * TERMS + k], h // PARTS, rows]
            if d:
                send_x(h, d).start()
        send_own(h).start()
        copy_own(h).start()

    pack_copy.wait()
    start_x(0)
    start_x(1)

    got = labels_out[x, 0:1] * 0
    spill = labels_out[NX, 0:1] * 0
    for d in range(1, NX * NC):
        label_from(d, 0).wait()
        label_from(d, 1).wait()
    for source in range(NX * NC):
        got = got + labels_in[0, source, 0:1]
        spill = spill + labels_in[1, source, 0:1]
    flags_out[...] = jnp.broadcast_to(spill, (8, LANES))

    def send_flag(d):
        return pltpu.make_async_remote_copy(
            src_ref=flags_out, dst_ref=flags_in.at[z],
            send_sem=gs_sem.at[d], recv_sem=gr_sem.at[z],
            device_id=at_z(d), device_id_type=MESH,
        )

    for d in range(1, NZ):
        send_flag(d).start()
    flags_in[z] = jnp.broadcast_to(spill, (8, LANES))

    ours = (got > 0) & ((got - 1) // 64 == core)
    goal_row = jnp.where(ours, (got - 1) % 64, 64)
    order_row = goal_row * LANES + row_iota((1, LANES), 1)
    goal = as_column(goal_row)
    order = goal * LANES + row_iota((LANES, 1), 0)
    before = order_row < order
    place = jnp.sum(jnp.where(before, 1, 0), axis=1, keepdims=True)
    follows = jnp.sum(jnp.where(before & (goal_row == goal), 1, 0), axis=1, keepdims=True)
    hit = place == lane
    number = row_iota((LANES, 1), 0)
    spot = (number // 16) * CAP + jnp.minimum(number % 16, CAP - 1)
    perm_row = jnp.sum(jnp.where(hit, spot, 0), axis=0, keepdims=True)
    same_row = jnp.sum(jnp.where(hit, jnp.minimum(follows, 1), 0), axis=0, keepdims=True)
    end_row = jnp.sum(jnp.where(goal <= lane, 1, 0), axis=0, keepdims=True)
    end_row = jnp.minimum(jnp.maximum(end_row - 1, 0), LANES - 1)
    some_row = jnp.sum(jnp.where(goal == lane, 1, 0), axis=0, keepdims=True)
    pick = row_iota((8, LANES), 0)
    plan_v[...] = jnp.where(
        pick == 0, perm_row, jnp.where(pick == 1, same_row, jnp.where(pick == 2, end_row, some_row))
    )
    plan_copy = pltpu.make_async_copy(plan_v, plan_s, sm_sem.at[1])
    plan_copy.start()

    loads[3].wait()

    def cycle(s, _):
        rows = jnp.concatenate([amp_ref[0, s], amp_ref[1, s]], axis=1)
        ints = ints_ref[blocks_ref[s]]
        prod = jnp.dot(rows, ints, preferred_element_type=jnp.float32)
        for j in range(8):
            ysend[j, s] = prod[:, j * TW : (j + 1) * TW].astype(jnp.bfloat16)
        return 0

    lax.fori_loop(0, SLOTS, cycle, 0)

    def send_y(d):
        return pltpu.make_async_remote_copy(
            src_ref=ysend.at[pl.ds(((y + d) % 4) * J, J)], dst_ref=yrecv.at[d],
            send_sem=ys_sem.at[d], recv_sem=yr_sem.at[d],
            device_id=at_y(d), device_id_type=MESH,
        )

    for d in range(1, 4):
        send_y(d).start()

    plan_copy.wait()

    def send_z(h, way, step):
        if step == 0:
            part = pl.ds(4 * way, 4)
        else:
            part = pl.ds(0, SLOTS)
        return pltpu.make_async_remote_copy(
            src_ref=zs.at[h, way, step, part], dst_ref=zr.at[h, way, step, part],
            send_sem=zs_sem.at[h, way, step], recv_sem=zr_sem.at[h, way, step],
            device_id=ups if way == 0 else downs, device_id_type=MESH,
        )

    def own(h, zz, s):
        goal = zz * SLOTS + s
        value = sums[h % RING, plan_s[2, goal]]
        return jnp.where(plan_s[3, goal] != 0, value, 0.0)

    def z_step(h, step):
        for way in range(2):
            if step > 0:
                send_z(h, way, step - 1).wait_recv()
            zz = (z + 4 - step) % NZ if way == 0 else (z + 4 + step) % NZ
            for s in range(4 * way, 4 * way + 4) if step == 0 else range(SLOTS):
                value = own(h, zz, s)
                if step > 1 or (step == 1 and s // 4 == way):
                    value = value + zr[h, way, step - 1, s].astype(jnp.float32)
                zs[h, way, step, s] = value.astype(jnp.bfloat16)
            send_z(h, way, step).start()

    def finish(h):
        rows = pl.ds((h % PARTS) * ROWS, ROWS)
        for way in range(2):
            send_z(h, way, 3).wait_recv()
        for s in range(SLOTS):
            total = own(h, z, s) + zr[h, 0, 3, s].astype(jnp.float32)
            total = total + zr[h, 1, 3, s].astype(jnp.float32)
            out_ref[h // PARTS, s, rows] = total

    def collect(h):
        for d in range(1, NX):
            arrived(h, ((x + d) % NX) * NC + core).wait()
            forward(h, d).start()
        copy_own(h).wait()
        for d in range(NX):
            arrived(h, ((x + d) % NX) * NC + 1 - core).wait()
        for source in range(NX * NC):
            stage[source * CAP : (source + 1) * CAP] = recv[h, source]

        def entry(e, total):
            value = stage[plan_s[0, e]].astype(jnp.float32)
            total = value + jnp.where(plan_s[1, e] != 0, total, 0.0)
            sums[h % RING, e] = total
            return total

        lax.fori_loop(0, NX * NC * CAP, entry, jnp.zeros((ROWS, TW), jnp.float32), unroll=4)

    def turn(i, _):
        @pl.when((i >= 1) & (i + 1 < CHUNKS))
        def _():
            start_x(i + 1)

        @pl.when(i < CHUNKS)
        def _():
            collect(i)
            z_step(i, 0)

        for step in range(1, 4):
            @pl.when((i >= step) & (i - step < CHUNKS))
            def _(step=step):
                z_step(i - step, step)

        @pl.when(i >= 4)
        def _():
            finish(i - 4)

        return 0

    lax.fori_loop(0, CHUNKS + 4, turn, 0)

    loads[4].wait()
    for d in range(1, 4):
        send_y(d).wait_recv()

    def add(s, _):
        for j in range(J):
            total = out_ref[j, s] + exch_ref[j, s].astype(jnp.float32)
            total = total + ysend[y * J + j, s].astype(jnp.float32)
            for d in range(1, 4):
                total = total + yrecv[d, j, s].astype(jnp.float32)
            out_ref[j, s] = total
        return 0

    lax.fori_loop(0, SLOTS, add, 0)

    flags = flags_in[z]
    for d in range(1, NZ):
        source = (z + d) % NZ
        pltpu.make_async_copy(flags_in.at[source], flags_in.at[source], gr_sem.at[source]).wait()
        flags = flags + flags_in[source]
    flag_ref[...] = flags

    for d in range(1, NX * NC):
        for which in range(2):
            send_label(d, which).wait_send()
    for d in range(1, NZ):
        send_flag(d).wait_send()
    for d in range(1, 4):
        send_y(d).wait_send()

    def drain(h, _):
        for d in range(1, NX):
            send_x(h, d).wait_send()
            forward(h, d).wait_send()
        send_own(h).wait_send()
        for way in range(2):
            for step in range(4):
                send_z(h, way, step).wait_send()
        return 0

    lax.fori_loop(0, CHUNKS, drain, 0)


def main_call(sources, factors, blocks, keys, amplitudes, exchange, left, right, ints):
    smem = pl.BlockSpec(memory_space=pltpu.SMEM)
    vmem = pl.BlockSpec(memory_space=pltpu.VMEM)
    hbm = pl.BlockSpec(memory_space=pl.ANY)
    dma = pltpu.SemaphoreType.DMA
    entries = NX * NC * CAP
    block = (J, SLOTS, TW, TW)
    return pl.pallas_call(
        main_kernel,
        out_shape=[
            jax.ShapeDtypeStruct(block, jnp.float32),
            jax.ShapeDtypeStruct((8, LANES), jnp.int32),
        ],
        in_specs=[smem, smem, smem, vmem, hbm, hbm, hbm, hbm, hbm],
        out_specs=[vmem, vmem],
        scratch_shapes=[
            pltpu.VMEM(block, jnp.bfloat16),
            pltpu.VMEM(block, jnp.bfloat16),
            pltpu.VMEM((16, TW, TW), jnp.bfloat16),
            pltpu.VMEM((16, TW, TW), jnp.bfloat16),
            pltpu.VMEM((2, 2 * TW, 8 * TW), jnp.bfloat16),
            pltpu.VMEM((16, TW, TW), jnp.bfloat16),
            pltpu.VMEM((TERMS, J, TW, TW), jnp.bfloat16),
            pltpu.VMEM((CHUNKS, NX, CAP, ROWS, TW), jnp.bfloat16),
            pltpu.VMEM((CHUNKS, NX * NC, CAP, ROWS, TW), jnp.bfloat16),
            pltpu.VMEM((entries, ROWS, TW), jnp.bfloat16),
            pltpu.VMEM((RING, LANES, ROWS, TW), jnp.float32),
            pltpu.VMEM((CHUNKS, 2, 4, SLOTS, ROWS, TW), jnp.bfloat16),
            pltpu.VMEM((CHUNKS, 2, 4, SLOTS, ROWS, TW), jnp.bfloat16),
            pltpu.VMEM((8, SLOTS, TW, TW), jnp.bfloat16),
            pltpu.VMEM((4,) + block, jnp.bfloat16),
            pltpu.VMEM((NX + 1, 8, LANES), jnp.int32),
            pltpu.VMEM((2, NX * NC, 8, LANES), jnp.int32),
            pltpu.VMEM((8, LANES), jnp.int32),
            pltpu.VMEM((NZ, 8, LANES), jnp.int32),
            pltpu.VMEM((8, LANES), jnp.int32),
            pltpu.VMEM((8, LANES), jnp.int32),
            pltpu.SMEM((8, LANES), jnp.int32),
            pltpu.SMEM((8, LANES), jnp.int32),
            dma((5,)),
            dma((CHUNKS, NX)),
            dma((CHUNKS, NX)),
            dma((CHUNKS,)),
            dma((CHUNKS, NX * NC)),
            dma((CHUNKS, 2, 4)),
            dma((CHUNKS, 2, 4)),
            dma((4,)),
            dma((4,)),
            dma((2, NX * NC)),
            dma((2, NX * NC)),
            dma((NZ,)),
            dma((NZ,)),
            dma((2,)),
        ],
        compiler_params=pltpu.CompilerParams(
            collective_id=0, has_side_effects=True, vmem_limit_bytes=58 * 2**20
        ),
        cost_estimate=pl.CostEstimate(
            flops=2 * 1024 * TW**3, bytes_accessed=8 * 2**20, transcendentals=0
        ),
    )(sources, factors, blocks, keys, amplitudes, exchange, left, right, ints)


def spilled(
    amplitudes, left_factors, right_factors, ladder_sources, ladder_factors, keys
):
    tile = lax.axis_index("tile")
    table = lax.all_gather(keys, "tile", axis=0)
    column, rank = ranks_in_column(keys)
    packed = ladder_terms(
        ladder_sources, ladder_factors, column * TERMS + rank, amplitudes, left_factors,
        right_factors,
    ).reshape(J, NX, TERMS, TW, TW)
    width = TERMS - CAP
    all_ranks = ranks_in_column(table)[1]
    group = (tile // 8) * 8
    here = lax.dynamic_slice_in_dim(table, group, 8, 0).reshape(-1)
    here_rank = lax.dynamic_slice_in_dim(all_ranks, group, 8, 0).reshape(-1)
    number = jnp.arange(8 * TERMS, dtype=jnp.int32)
    valid = ((here // SLOTS) % 8 == tile % 8) & (here_rank >= CAP)
    target = jnp.where(valid, (here // (SLOTS * 8)) * SLOTS + here % SLOTS, 64)
    order = target * 256 + number
    place = jnp.sum((order[None, :] < order[:, None]).astype(jnp.int32), axis=1)
    hit = place[None, :] == number[:, None]
    spot = (number // TERMS) * width + jnp.maximum(here_rank - CAP, 0)
    perm = jnp.sum(jnp.where(hit, spot[None, :], 0), axis=1)
    sorted_target = jnp.sum(jnp.where(hit, target[None, :], 0), axis=1)
    same = jnp.concatenate(
        [jnp.zeros((1,), jnp.int32), (sorted_target[1:] == sorted_target[:-1]).astype(jnp.int32)]
    )
    goal = jnp.arange(64, dtype=jnp.int32)[:, None]
    end = jnp.maximum(jnp.sum((target[None, :] <= goal).astype(jnp.int32), axis=1) - 1, 0)
    some = jnp.sum((target[None, :] == goal).astype(jnp.int32), axis=1)
    entries = 8 * width
    return route(CAP, width, entries, 1, perm[:entries], same[:entries], end, some, packed)


def local(
    amplitudes, exchange_ints, left_factors, right_factors, ladder_sources, ladder_factors,
    dest_owners, dest_slots, cycle_blocks, cycle_ints,
):
    keys = dest_owners[:, 0] * SLOTS + dest_slots
    row = jnp.pad(keys, (0, LANES - TERMS))[None, :]
    total, flags = main_call(
        ladder_sources, ladder_factors, cycle_blocks, row, amplitudes, exchange_ints,
        left_factors, right_factors, cycle_ints,
    )

    def whole():
        return total.astype(jnp.bfloat16)

    def more():
        rest = spilled(
            amplitudes, left_factors, right_factors, ladder_sources, ladder_factors, keys
        )
        return (total + rest).astype(jnp.bfloat16)

    return lax.cond(jnp.max(flags) > 0, more, whole)


def solution(mesh):
    placed = (
        P("occ", "tile", None, None),
        P("occ", "tile", None, None),
        P("tile", None, None),
        P("tile", None, None),
        P("tile", None),
        P("tile", None),
        P("tile", None),
        P("tile"),
        P("tile"),
        P("tile", "occ", None),
    )
    return jax.shard_map(
        local, mesh=mesh, in_specs=placed, out_specs=P("occ", "tile", None, None), check_vma=False
    )
```

```python
import functools

import jax
import jax.numpy as jnp
from jax import lax
from jax.experimental import pallas as pl
from jax.experimental.pallas import tpu as pltpu
from jax.sharding import PartitionSpec as P

MESH = pl.DeviceIdType.MESH
NZ, NX, NC = 8, 4, 2
TERMS = 32
SLOTS = 8
TW = 128
J = 2
ROWS = 32
PARTS = TW // ROWS
CHUNKS = J * PARTS
RING = 5
CAP = 14
LANES = 128
LAG = 1
HALF = 16
QUARTERS = TW // 2 // HALF
STEPS = J * QUARTERS
GOALS = NC * SLOTS


def ladder_kernel(src_ref, fac_ref, pos_ref, amp_ref, left_ref, right_ref, out_ref, rt, stage, sem):
    for f in range(16):
        rt[f] = right_ref[f].T

    def put(g):
        return pltpu.make_async_copy(stage.at[g], out_ref.at[:, pos_ref[g]], sem.at[g])

    def one(g, _):
        acc = jnp.zeros((2 * TW, TW), jnp.float32)
        for q in range(8):
            s = src_ref[g, q]
            f = fac_ref[g, q]
            amps = jnp.concatenate([amp_ref[0, s], amp_ref[1, s]], axis=1)
            half = jnp.dot(left_ref[f], amps, preferred_element_type=jnp.float32).astype(
                jnp.bfloat16
            )
            both = jnp.concatenate([half[:, :TW], half[:, TW:]], axis=0)
            acc = acc + jnp.dot(both, rt[f], preferred_element_type=jnp.float32)
        stage[g] = acc.astype(jnp.bfloat16).reshape(J, TW, TW)
        put(g).start()
        return 0

    lax.fori_loop(0, TERMS, one, 0)

    def finish(g, _):
        put(g).wait()
        return 0

    lax.fori_loop(0, TERMS, finish, 0)


def ladder_terms(sources, factors, places, amplitudes, left, right):
    smem = pl.BlockSpec(memory_space=pltpu.SMEM)
    vmem = pl.BlockSpec(memory_space=pltpu.VMEM)
    return pl.pallas_call(
        ladder_kernel,
        out_shape=jax.ShapeDtypeStruct((J, NX * TERMS, TW, TW), jnp.bfloat16),
        in_specs=[smem, smem, smem, vmem, vmem, vmem],
        out_specs=pl.BlockSpec(memory_space=pl.ANY),
        scratch_shapes=[
            pltpu.VMEM((16, TW, TW), jnp.bfloat16),
            pltpu.VMEM((TERMS, J, TW, TW), jnp.bfloat16),
            pltpu.SemaphoreType.DMA((TERMS,)),
        ],
        compiler_params=pltpu.CompilerParams(vmem_limit_bytes=32 * 2**20),
        cost_estimate=pl.CostEstimate(
            flops=2 * 1024 * TW**3, bytes_accessed=4 * 2**20, transcendentals=0
        ),
    )(sources, factors, places, amplitudes, left, right)


def route_kernel(
    first, cap, entries, perm_ref, same_ref, end_ref, some_ref, p_ref, out_ref,
    recv, stage, sums, zs, zr, xs_sem, fs_sem, lx_sem, rx_sem, zs_sem, zr_sem,
):
    t = lax.axis_index("tile")
    y = lax.axis_index("occ")
    core = t % NC
    x = (t // NC) % NX
    z = t // (NC * NX)
    m = t % (NC * NX)

    def at(zz, xx, cc):
        return {"tile": (zz * NX + xx) * NC + cc, "occ": y}

    sibling = at(z, x, 1 - core)
    ups = at((z + 1) % NZ, x, core)
    downs = at((z + NZ - 1) % NZ, x, core)
    barrier = pltpu.get_barrier_semaphore()
    partners = [at(z, (x + d) % NX, core) for d in range(1, NX)] + [sibling, ups, downs]
    for partner in partners:
        pl.semaphore_signal(barrier, inc=1, device_id=partner, device_id_type=MESH)
    pl.semaphore_wait(barrier, len(partners))

    def mine(h, xx):
        return p_ref.at[h // PARTS, xx, pl.ds(first, cap), pl.ds((h % PARTS) * ROWS, ROWS)]

    def send_x(h, d):
        xx = (x + d) % NX
        return pltpu.make_async_remote_copy(
            src_ref=mine(h, xx), dst_ref=recv.at[h, m],
            send_sem=xs_sem.at[h, d], recv_sem=rx_sem.at[h, m],
            device_id=at(z, xx, core), device_id_type=MESH,
        )

    def send_own(h):
        return pltpu.make_async_remote_copy(
            src_ref=mine(h, x), dst_ref=recv.at[h, m],
            send_sem=xs_sem.at[h, 0], recv_sem=rx_sem.at[h, m],
            device_id=sibling, device_id_type=MESH,
        )

    def copy_own(h):
        return pltpu.make_async_copy(mine(h, x), recv.at[h, m], lx_sem.at[h])

    def forward(h, d):
        source = ((x + d) % NX) * NC + core
        return pltpu.make_async_remote_copy(
            src_ref=recv.at[h, source], dst_ref=recv.at[h, source],
            send_sem=fs_sem.at[h, d], recv_sem=rx_sem.at[h, source],
            device_id=sibling, device_id_type=MESH,
        )

    def arrived(h, source):
        return pltpu.make_async_copy(recv.at[h, source], recv.at[h, source], rx_sem.at[h, source])

    def start_x(h):
        for d in range(1, NX):
            send_x(h, d).start()
        send_own(h).start()
        copy_own(h).start()

    def send_z(h, way, step):
        if step == 0:
            part = pl.ds(4 * way, 4)
        else:
            part = pl.ds(0, SLOTS)
        return pltpu.make_async_remote_copy(
            src_ref=zs.at[h, way, step, part], dst_ref=zr.at[h, way, step, part],
            send_sem=zs_sem.at[h, way, step], recv_sem=zr_sem.at[h, way, step],
            device_id=ups if way == 0 else downs, device_id_type=MESH,
        )

    def own(h, zz, s):
        place = zz * SLOTS + s
        value = sums[h % RING, end_ref[place]]
        return jnp.where(some_ref[place] != 0, value, 0.0)

    def z_step(h, step):
        for way in range(2):
            if step > 0:
                send_z(h, way, step - 1).wait_recv()
            zz = (z + 4 - step) % NZ if way == 0 else (z + 4 + step) % NZ
            for s in range(4 * way, 4 * way + 4) if step == 0 else range(SLOTS):
                value = own(h, zz, s)
                if step > 1 or (step == 1 and s // 4 == way):
                    value = value + zr[h, way, step - 1, s].astype(jnp.float32)
                zs[h, way, step, s] = value.astype(jnp.bfloat16)
            send_z(h, way, step).start()

    def finish(h):
        for way in range(2):
            send_z(h, way, 3).wait_recv()
        for s in range(SLOTS):
            total = own(h, z, s) + zr[h, 0, 3, s].astype(jnp.float32)
            total = total + zr[h, 1, 3, s].astype(jnp.float32)
            out_ref[h // PARTS, s, pl.ds((h % PARTS) * ROWS, ROWS)] = total

    def collect(h):
        for d in range(1, NX):
            arrived(h, ((x + d) % NX) * NC + core).wait()
            forward(h, d).start()
        copy_own(h).wait()
        for d in range(NX):
            arrived(h, ((x + d) % NX) * NC + 1 - core).wait()
        for source in range(NX * NC):
            stage[source * cap : (source + 1) * cap] = recv[h, source]

        def entry(e, total):
            value = stage[perm_ref[e]].astype(jnp.float32)
            total = value + jnp.where(same_ref[e] != 0, total, 0.0)
            sums[h % RING, e] = total
            return total

        lax.fori_loop(0, entries, entry, jnp.zeros((ROWS, TW), jnp.float32), unroll=4)

    start_x(0)

    def turn(i, _):
        @pl.when(i + 1 < CHUNKS)
        def _():
            start_x(i + 1)

        @pl.when(i < CHUNKS)
        def _():
            collect(i)
            z_step(i, 0)

        for step in range(1, 4):
            @pl.when((i >= step) & (i - step < CHUNKS))
            def _(step=step):
                z_step(i - step, step)

        @pl.when(i >= 4)
        def _():
            finish(i - 4)

        return 0

    lax.fori_loop(0, CHUNKS + 4, turn, 0)

    def drain(h, _):
        for d in range(1, NX):
            send_x(h, d).wait_send()
            forward(h, d).wait_send()
        send_own(h).wait_send()
        for way in range(2):
            for step in range(4):
                send_z(h, way, step).wait_send()
        return 0

    lax.fori_loop(0, CHUNKS, drain, 0)


def route(first, cap, entries, collective_id, perm, same, end, some, packed):
    smem = pl.BlockSpec(memory_space=pltpu.SMEM)
    dma = pltpu.SemaphoreType.DMA
    return pl.pallas_call(
        functools.partial(route_kernel, first, cap, entries),
        out_shape=jax.ShapeDtypeStruct((J, SLOTS, TW, TW), jnp.float32),
        in_specs=[smem, smem, smem, smem, pl.BlockSpec(memory_space=pl.ANY)],
        out_specs=pl.BlockSpec(memory_space=pltpu.VMEM),
        scratch_shapes=[
            pltpu.VMEM((CHUNKS, NX * NC, cap, ROWS, TW), jnp.bfloat16),
            pltpu.VMEM((NX * NC * cap, ROWS, TW), jnp.bfloat16),
            pltpu.VMEM((RING, entries, ROWS, TW), jnp.float32),
            pltpu.VMEM((CHUNKS, 2, 4, SLOTS, ROWS, TW), jnp.bfloat16),
            pltpu.VMEM((CHUNKS, 2, 4, SLOTS, ROWS, TW), jnp.bfloat16),
            dma((CHUNKS, NX)),
            dma((CHUNKS, NX)),
            dma((CHUNKS,)),
            dma((CHUNKS, NX * NC)),
            dma((CHUNKS, 2, 4)),
            dma((CHUNKS, 2, 4)),
        ],
        compiler_params=pltpu.CompilerParams(
            collective_id=collective_id, has_side_effects=True, vmem_limit_bytes=56 * 2**20
        ),
        cost_estimate=pl.CostEstimate(
            flops=2**22, bytes_accessed=8 * 2**20, transcendentals=0
        ),
    )(perm, same, end, some, packed)


def ranks_in_column(keys):
    column = (keys // (SLOTS * NC)) % NX
    order = jnp.arange(TERMS, dtype=jnp.int32)
    earlier = order[:, None] > order[None, :]
    alike = column[..., :, None] == column[..., None, :]
    return column, jnp.sum((alike & earlier).astype(jnp.int32), axis=-1)


def row_iota(shape, axis):
    return lax.broadcasted_iota(jnp.int32, shape, axis)


def as_column(row):
    diagonal = row_iota((LANES, LANES), 0) == row_iota((LANES, LANES), 1)
    return jnp.sum(jnp.where(diagonal, row, 0), axis=1, keepdims=True)


def main_kernel(
    blocks_ref, owners_ref, slots_ref, src_hbm, fac_hbm, amp_hbm, exch_hbm, left_hbm, right_hbm, ints_hbm,
    out_ref, flag_ref,
    src_ref, fac_ref, keys_v, amp_ref, exch_ref, left_ref, right_ref, ints_ref, rt, terms, packed, recv, stage, sums,
    zs, zr, ysend, yrecv, fsend, frecv, labels_out, labels_in, flags_out, flags_in,
    pack_v, plan_v, pack_s, plan_s, flag_s,
    in_sem, xs_sem, lx_sem, rx_sem, zs_sem, zr_sem, ys_sem, yr_sem, ls_sem, lr_sem,
    gs_sem, gr_sem, sm_sem, es_sem, er_sem,
):
    t = lax.axis_index("tile")
    y = lax.axis_index("occ")
    core = t % NC
    x = (t // NC) % NX
    z = t // (NC * NX)
    m = t % (NC * NX)

    def at(zz, xx, cc):
        return {"tile": (zz * NX + xx) * NC + cc, "occ": y}

    def at_y(d):
        return {"tile": t, "occ": (y + d) % 4}

    def at_m(d):
        return {"tile": z * (NX * NC) + (m + d) % (NX * NC), "occ": y}

    def at_z(d):
        return at((z + d) % NZ, x, core)

    sibling = at(z, x, 1 - core)
    ups = at_z(1)
    downs = at_z(NZ - 1)

    loads = [
        pltpu.make_async_copy(hbm, ref, in_sem.at[n])
        for n, (hbm, ref) in enumerate(
            [(right_hbm, right_ref), (left_hbm, left_ref), (amp_hbm, amp_ref),
             (ints_hbm, ints_ref), (exch_hbm, exch_ref), (src_hbm, src_ref), (fac_hbm, fac_ref)]
        )
    ]
    for load in loads:
        load.start()

    barrier = pltpu.get_barrier_semaphore()
    partners = [at_m(d) for d in range(1, NX * NC)] + [at_z(d) for d in range(1, NZ)]
    partners = partners + [at_y(d) for d in range(1, 4)]
    for partner in partners:
        pl.semaphore_signal(barrier, inc=1, device_id=partner, device_id_type=MESH)

    lane = row_iota((LANES, LANES), 1)
    line = row_iota((LANES, LANES), 0)
    keys_v[...] = jnp.zeros((8, LANES), jnp.int32)
    keys_v[0:1, 0:TERMS] = owners_ref[...] * SLOTS + slots_ref[...]
    keys = keys_v[0:1]
    key_column = as_column(keys)
    real = line < TERMS
    column_row = jnp.where(row_iota((1, LANES), 1) < TERMS, (keys // 16) % NX, NX)
    column = (key_column // 16) % NX
    rank = jnp.sum(
        jnp.where((column_row == column) & (lane < line), 1, 0), axis=1, keepdims=True
    )
    pack_v[...] = jnp.broadcast_to(
        jnp.sum(jnp.where(real & (column * TERMS + rank == lane), line, 0), axis=0, keepdims=True),
        (8, LANES),
    )
    label = ((key_column // 8) % NC) * 64 + (key_column // 64) * SLOTS + key_column % SLOTS
    for xx in range(NX):
        here = real & (column == xx) & (rank < CAP) & (m * 16 + rank == lane)
        row = jnp.sum(jnp.where(here, label + 1, 0), axis=0, keepdims=True)
        labels_out[xx] = jnp.broadcast_to(row, (8, LANES))
    over = jnp.max(jnp.where(real & (rank >= CAP), 1, 0), axis=0, keepdims=True)
    labels_out[NX] = jnp.broadcast_to(over, (8, LANES))
    pack_copy = pltpu.make_async_copy(pack_v, pack_s, sm_sem.at[0])
    pack_copy.start()

    pl.semaphore_wait(barrier, len(partners))

    def send_label(d, which):
        if which == 0:
            part = (((m + d) % (NX * NC)) // NC)
        else:
            part = NX
        return pltpu.make_async_remote_copy(
            src_ref=labels_out.at[part], dst_ref=labels_in.at[which, m],
            send_sem=ls_sem.at[which, d], recv_sem=lr_sem.at[which, m],
            device_id=at_m(d), device_id_type=MESH,
        )

    def label_from(d, which):
        source = (m + d) % (NX * NC)
        return pltpu.make_async_copy(
            labels_in.at[which, source], labels_in.at[which, source], lr_sem.at[which, source]
        )

    for d in range(1, NX * NC):
        for which in range(2):
            send_label(d, which).start()
    labels_in[0, m] = labels_out[x]
    labels_in[1, m] = labels_out[NX]

    loads[0].wait()
    for f in range(16):
        rt[f] = right_ref[f].T
    loads[1].wait()
    loads[2].wait()

    loads[5].wait()
    loads[6].wait()

    def one(g, j):
        halves, rights = [], []
        for q in range(8):
            f = fac_ref[q, g]
            half = jnp.dot(
                left_ref[f], amp_ref[j, src_ref[q, g]], preferred_element_type=jnp.float32
            )
            halves.append(half.astype(jnp.bfloat16))
            rights.append(rt[f])
        acc = jnp.dot(
            jnp.concatenate(halves, axis=1), jnp.concatenate(rights, axis=0),
            preferred_element_type=jnp.float32,
        )
        terms[j, g] = acc.astype(jnp.bfloat16)
        return j

    lax.fori_loop(0, TERMS, one, 0, unroll=4)

    def send_x(h, d, cc):
        to = at(z, (x + d) % NX, cc)
        return pltpu.make_async_remote_copy(
            src_ref=packed.at[h, (x + d) % NX, cc], dst_ref=recv.at[h, m],
            send_sem=xs_sem.at[h, d, cc], recv_sem=rx_sem.at[h, m],
            device_id=to, device_id_type=MESH,
        )

    def send_own(h):
        return pltpu.make_async_remote_copy(
            src_ref=packed.at[h, x, 1 - core], dst_ref=recv.at[h, m],
            send_sem=xs_sem.at[h, 0, 0], recv_sem=rx_sem.at[h, m],
            device_id=sibling, device_id_type=MESH,
        )

    def copy_own(h):
        return pltpu.make_async_copy(packed.at[h, x, core], recv.at[h, m], lx_sem.at[h])

    def arrived(h, source):
        return pltpu.make_async_copy(recv.at[h, source], recv.at[h, source], rx_sem.at[h, source])

    def start_x(h):
        for d in (2, 1, 3, 0):
            xx = (x + d) % NX
            for cc in range(NC):
                rows = pl.ds(cc * (TW // 2) + (h % QUARTERS) * HALF, HALF)
                for k in range(CAP):
                    packed[h, xx, cc, k] = terms[h // QUARTERS, pack_s[0, xx * TERMS + k], rows]
            if d:
                for cc in range(NC):
                    send_x(h, d, cc).start()
        send_own(h).start()
        copy_own(h).start()

    pack_copy.wait()
    start_x(0)
    lax.fori_loop(0, TERMS, one, 1, unroll=4)
    start_x(1)

    got = labels_out[x, 0:1] * 0
    spill = labels_out[NX, 0:1] * 0
    for d in range(1, NX * NC):
        label_from(d, 0).wait()
        label_from(d, 1).wait()
    for source in range(NX * NC):
        got = got + labels_in[0, source, 0:1]
        spill = spill + labels_in[1, source, 0:1]
    flags_out[...] = jnp.broadcast_to(spill, (8, LANES))

    def send_flag(d):
        return pltpu.make_async_remote_copy(
            src_ref=flags_out, dst_ref=flags_in.at[z],
            send_sem=gs_sem.at[d], recv_sem=gr_sem.at[z],
            device_id=at_z(d), device_id_type=MESH,
        )

    for d in range(1, NZ):
        send_flag(d).start()
    flags_in[z] = jnp.broadcast_to(spill, (8, LANES))

    goal_row = jnp.where(got > 0, got - 1, LANES)
    order_row = goal_row * LANES + row_iota((1, LANES), 1)
    goal = as_column(goal_row)
    order = goal * LANES + row_iota((LANES, 1), 0)
    before = order_row < order
    place = jnp.sum(jnp.where(before, 1, 0), axis=1, keepdims=True)
    follows = jnp.sum(jnp.where(before & (goal_row == goal), 1, 0), axis=1, keepdims=True)
    hit = place == lane
    number = row_iota((LANES, 1), 0)
    spot = (number // 16) * CAP + jnp.minimum(number % 16, CAP - 1)
    perm_row = jnp.sum(jnp.where(hit, spot, 0), axis=0, keepdims=True)
    same_row = jnp.sum(jnp.where(hit, jnp.minimum(follows, 1), 0), axis=0, keepdims=True)
    end_row = jnp.sum(jnp.where(goal <= lane, 1, 0), axis=0, keepdims=True)
    end_row = jnp.minimum(jnp.maximum(end_row - 1, 0), NX * NC * CAP - 1)
    some_row = jnp.sum(jnp.where(goal == lane, 1, 0), axis=0, keepdims=True)
    pick = row_iota((8, LANES), 0)
    plan_v[...] = jnp.where(
        pick == 0, perm_row, jnp.where(pick == 1, same_row, jnp.where(pick == 2, end_row, some_row))
    )
    plan_copy = pltpu.make_async_copy(plan_v, plan_s, sm_sem.at[1])
    plan_copy.start()

    def cycle(s, _):
        rows = jnp.concatenate([amp_ref[0, s], amp_ref[1, s]], axis=1)
        ints = ints_ref[blocks_ref[s]]
        prod = jnp.dot(rows, ints, preferred_element_type=jnp.float32)
        for j in range(8):
            ysend[j, s] = prod[:, j * TW : (j + 1) * TW].astype(jnp.bfloat16)
        return 0

    def send_y(d):
        return pltpu.make_async_remote_copy(
            src_ref=ysend.at[pl.ds(((y + d) % 4) * J, J)], dst_ref=yrecv.at[d],
            send_sem=ys_sem.at[d], recv_sem=yr_sem.at[d],
            device_id=at_y(d), device_id_type=MESH,
        )

    plan_copy.wait()

    def send_z(h, way, step):
        if step == 0:
            part = pl.ds(SLOTS * way, SLOTS)
        else:
            part = pl.ds(0, GOALS)
        return pltpu.make_async_remote_copy(
            src_ref=zs.at[h, way, step, part], dst_ref=zr.at[h, way, step, part],
            send_sem=zs_sem.at[h, way, step], recv_sem=zr_sem.at[h, way, step],
            device_id=ups if way == 0 else downs, device_id_type=MESH,
        )

    def own(h, zz, n):
        goal = (n // SLOTS) * 64 + zz * SLOTS + n % SLOTS
        value = sums[h, plan_s[2, goal]]
        return jnp.where(plan_s[3, goal] != 0, value, 0.0)

    def z_step(h, step):
        for way in range(2):
            if step > 0:
                send_z(h, way, step - 1).wait_recv()
            zz = (z + 4 - step) % NZ if way == 0 else (z + 4 + step) % NZ
            for n in range(SLOTS * way, SLOTS * way + SLOTS) if step == 0 else range(GOALS):
                value = own(h, zz, n)
                if step > 1 or (step == 1 and n // SLOTS == way):
                    value = value + zr[h, way, step - 1, n].astype(jnp.float32)
                zs[h, way, step, n] = value.astype(jnp.bfloat16)
            send_z(h, way, step).start()

    def send_end(h):
        return pltpu.make_async_remote_copy(
            src_ref=fsend.at[h], dst_ref=frecv.at[h], send_sem=es_sem.at[h],
            recv_sem=er_sem.at[h], device_id=sibling, device_id_type=MESH,
        )

    def finish(h):
        for way in range(2):
            send_z(h, way, 3).wait_recv()

        def total(cc, s):
            n = cc * SLOTS + s
            value = own(h, z, n) + zr[h, 0, 3, n].astype(jnp.float32)
            return value + zr[h, 1, 3, n].astype(jnp.float32)

        for s in range(SLOTS):
            fsend[h, s] = total(1 - core, s)
        send_end(h).start()
        rows = pl.ds(core * (TW // 2) + (h % QUARTERS) * HALF, HALF)
        for s in range(SLOTS):
            out_ref[h // QUARTERS, s, rows] = total(core, s)

    def collect(h):
        copy_own(h).wait()
        for d in range(1, NX * NC):
            arrived(h, (m + d) % (NX * NC)).wait()
        for source in range(NX * NC):
            stage[source * CAP : (source + 1) * CAP] = recv[h, source]

        def entry(e, total):
            value = stage[plan_s[0, e]].astype(jnp.float32)
            total = value + jnp.where(plan_s[1, e] != 0, total, 0.0)
            sums[h, e] = total
            return total

        lax.fori_loop(0, NX * NC * CAP, entry, jnp.zeros((HALF, TW), jnp.float32), unroll=8)

    def turn(i, _):
        @pl.when(i + 2 < STEPS)
        def _():
            start_x(i + 2)

        @pl.when(i < STEPS)
        def _():
            collect(i)
            z_step(i, 0)

        for step in range(1, 4):
            @pl.when((i >= LAG * step) & (i - LAG * step < STEPS))
            def _(step=step):
                z_step(i - LAG * step, step)

        @pl.when(i < 2)
        def _():
            @pl.when(i == 0)
            def _():
                loads[3].wait()

            lax.fori_loop(i * 4, i * 4 + 4, cycle, 0)

            @pl.when(i == 1)
            def _():
                for d in range(1, 4):
                    send_y(d).start()

        @pl.when(i >= LAG * 4)
        def _():
            finish(i - LAG * 4)

        return 0

    lax.fori_loop(0, STEPS + LAG * 4, turn, 0)

    def ending(h, _):
        send_end(h).wait_recv()
        rows = pl.ds((1 - core) * (TW // 2) + (h % QUARTERS) * HALF, HALF)
        for s in range(SLOTS):
            out_ref[h // QUARTERS, s, rows] = frecv[h, s]
        return 0

    lax.fori_loop(0, STEPS, ending, 0)

    loads[4].wait()
    for d in range(1, 4):
        send_y(d).wait_recv()

    def add(s, _):
        for j in range(J):
            total = out_ref[j, s] + exch_ref[j, s].astype(jnp.float32)
            total = total + ysend[y * J + j, s].astype(jnp.float32)
            for d in range(1, 4):
                total = total + yrecv[d, j, s].astype(jnp.float32)
            out_ref[j, s] = total
        return 0

    lax.fori_loop(0, SLOTS, add, 0)

    flags = flags_in[z]
    for d in range(1, NZ):
        source = (z + d) % NZ
        pltpu.make_async_copy(flags_in.at[source], flags_in.at[source], gr_sem.at[source]).wait()
        flags = flags + flags_in[source]
    pack_v[...] = jnp.broadcast_to(jnp.max(flags, axis=1, keepdims=True), (8, LANES))
    flag_copy = pltpu.make_async_copy(pack_v, flag_s, sm_sem.at[2])
    flag_copy.start()

    for d in range(1, NX * NC):
        for which in range(2):
            send_label(d, which).wait_send()
    for d in range(1, NZ):
        send_flag(d).wait_send()
    for d in range(1, 4):
        send_y(d).wait_send()

    def drain(h, _):
        for d in range(1, NX):
            for cc in range(NC):
                send_x(h, d, cc).wait_send()
        send_own(h).wait_send()
        send_end(h).wait_send()
        for way in range(2):
            for step in range(4):
                send_z(h, way, step).wait_send()
        return 0

    lax.fori_loop(0, STEPS, drain, 0)
    flag_copy.wait()
    flag_ref[0] = flag_s[0, 0]


def main_call(sources, factors, blocks, owners, slots, amplitudes, exchange, left, right, ints):
    smem = pl.BlockSpec(memory_space=pltpu.SMEM)
    vmem = pl.BlockSpec(memory_space=pltpu.VMEM)
    hbm = pl.BlockSpec(memory_space=pl.ANY)
    dma = pltpu.SemaphoreType.DMA
    entries = NX * NC * CAP
    block = (J, SLOTS, TW, TW)
    return pl.pallas_call(
        main_kernel,
        out_shape=[
            jax.ShapeDtypeStruct(block, jnp.float32),
            jax.ShapeDtypeStruct((1,), jnp.int32),
        ],
        in_specs=[smem, vmem, vmem] + [hbm] * 7,
        out_specs=[vmem, smem],
        scratch_shapes=[
            pltpu.SMEM((8, TERMS), jnp.int32),
            pltpu.SMEM((8, TERMS), jnp.int32),
            pltpu.VMEM((8, LANES), jnp.int32),
            pltpu.VMEM(block, jnp.bfloat16),
            pltpu.VMEM(block, jnp.bfloat16),
            pltpu.VMEM((16, TW, TW), jnp.bfloat16),
            pltpu.VMEM((16, TW, TW), jnp.bfloat16),
            pltpu.VMEM((2, 2 * TW, 8 * TW), jnp.bfloat16),
            pltpu.VMEM((16, TW, TW), jnp.bfloat16),
            pltpu.VMEM((J, TERMS, TW, TW), jnp.bfloat16),
            pltpu.VMEM((STEPS, NX, NC, CAP, HALF, TW), jnp.bfloat16),
            pltpu.VMEM((STEPS, NX * NC, CAP, HALF, TW), jnp.bfloat16),
            pltpu.VMEM((entries, HALF, TW), jnp.bfloat16),
            pltpu.VMEM((STEPS, entries, HALF, TW), jnp.float32),
            pltpu.VMEM((STEPS, 2, 4, GOALS, HALF, TW), jnp.bfloat16),
            pltpu.VMEM((STEPS, 2, 4, GOALS, HALF, TW), jnp.bfloat16),
            pltpu.VMEM((8, SLOTS, TW, TW), jnp.bfloat16),
            pltpu.VMEM((4,) + block, jnp.bfloat16),
            pltpu.VMEM((STEPS, SLOTS, HALF, TW), jnp.float32),
            pltpu.VMEM((STEPS, SLOTS, HALF, TW), jnp.float32),
            pltpu.VMEM((NX + 1, 8, LANES), jnp.int32),
            pltpu.VMEM((2, NX * NC, 8, LANES), jnp.int32),
            pltpu.VMEM((8, LANES), jnp.int32),
            pltpu.VMEM((NZ, 8, LANES), jnp.int32),
            pltpu.VMEM((8, LANES), jnp.int32),
            pltpu.VMEM((8, LANES), jnp.int32),
            pltpu.SMEM((8, LANES), jnp.int32),
            pltpu.SMEM((8, LANES), jnp.int32),
            pltpu.SMEM((8, LANES), jnp.int32),
            dma((7,)),
            dma((STEPS, NX, NC)),
            dma((STEPS,)),
            dma((STEPS, NX * NC)),
            dma((STEPS, 2, 4)),
            dma((STEPS, 2, 4)),
            dma((4,)),
            dma((4,)),
            dma((2, NX * NC)),
            dma((2, NX * NC)),
            dma((NZ,)),
            dma((NZ,)),
            dma((3,)),
            dma((STEPS,)),
            dma((STEPS,)),
        ],
        compiler_params=pltpu.CompilerParams(
            collective_id=0, has_side_effects=True, vmem_limit_bytes=58 * 2**20
        ),
        cost_estimate=pl.CostEstimate(
            flops=2 * 1024 * TW**3, bytes_accessed=8 * 2**20, transcendentals=0
        ),
    )(blocks, owners, slots, sources, factors, amplitudes, exchange, left, right, ints)


def spilled(
    amplitudes, left_factors, right_factors, ladder_sources, ladder_factors, keys
):
    tile = lax.axis_index("tile")
    table = lax.all_gather(keys, "tile", axis=0)
    column, rank = ranks_in_column(keys)
    packed = ladder_terms(
        ladder_sources, ladder_factors, column * TERMS + rank, amplitudes, left_factors,
        right_factors,
    ).reshape(J, NX, TERMS, TW, TW)
    width = TERMS - CAP
    all_ranks = ranks_in_column(table)[1]
    group = (tile // 8) * 8
    here = lax.dynamic_slice_in_dim(table, group, 8, 0).reshape(-1)
    here_rank = lax.dynamic_slice_in_dim(all_ranks, group, 8, 0).reshape(-1)
    number = jnp.arange(8 * TERMS, dtype=jnp.int32)
    valid = ((here // SLOTS) % 8 == tile % 8) & (here_rank >= CAP)
    target = jnp.where(valid, (here // (SLOTS * 8)) * SLOTS + here % SLOTS, 64)
    order = target * 256 + number
    place = jnp.sum((order[None, :] < order[:, None]).astype(jnp.int32), axis=1)
    hit = place[None, :] == number[:, None]
    spot = (number // TERMS) * width + jnp.maximum(here_rank - CAP, 0)
    perm = jnp.sum(jnp.where(hit, spot[None, :], 0), axis=1)
    sorted_target = jnp.sum(jnp.where(hit, target[None, :], 0), axis=1)
    same = jnp.concatenate(
        [jnp.zeros((1,), jnp.int32), (sorted_target[1:] == sorted_target[:-1]).astype(jnp.int32)]
    )
    goal = jnp.arange(64, dtype=jnp.int32)[:, None]
    end = jnp.maximum(jnp.sum((target[None, :] <= goal).astype(jnp.int32), axis=1) - 1, 0)
    some = jnp.sum((target[None, :] == goal).astype(jnp.int32), axis=1)
    entries = 8 * width
    return route(CAP, width, entries, 1, perm[:entries], same[:entries], end, some, packed)


def local(
    amplitudes, exchange_ints, left_factors, right_factors, ladder_sources, ladder_factors,
    dest_owners, dest_slots, cycle_blocks, cycle_ints,
):
    total, flags = main_call(
        ladder_sources.T, ladder_factors.T, cycle_blocks, dest_owners.reshape(1, TERMS),
        dest_slots[None, :], amplitudes, exchange_ints,
        left_factors, right_factors, cycle_ints,
    )

    def whole():
        return total.astype(jnp.bfloat16)

    def more():
        keys = dest_owners[:, 0] * SLOTS + dest_slots
        rest = spilled(
            amplitudes, left_factors, right_factors, ladder_sources, ladder_factors, keys
        )
        return (total + rest).astype(jnp.bfloat16)

    return lax.cond(flags[0] > 0, more, whole)


def solution(mesh):
    placed = (
        P("occ", "tile", None, None),
        P("occ", "tile", None, None),
        P("tile", None, None),
        P("tile", None, None),
        P("tile", None),
        P("tile", None),
        P("tile", None),
        P("tile"),
        P("tile"),
        P("tile", "occ", None),
    )
    return jax.shard_map(
        local, mesh=mesh, in_specs=placed, out_specs=P("occ", "tile", None, None), check_vma=False
    )
```

```python
import functools

import jax
import jax.numpy as jnp
from jax import lax
from jax.experimental import pallas as pl
from jax.experimental.pallas import tpu as pltpu
from jax.sharding import PartitionSpec as P

MESH = pl.DeviceIdType.MESH
NZ, NX, NC = 8, 4, 2
TERMS = 32
SLOTS = 8
TW = 128
J = 2
ROWS = 32
PARTS = TW // ROWS
CHUNKS = J * PARTS
RING = 5
CAP = 14
LANES = 128
HALF = 16
QUARTERS = TW // 2 // HALF
STEPS = J * QUARTERS
GOALS = NC * SLOTS


def ladder_kernel(src_ref, fac_ref, pos_ref, amp_ref, left_ref, right_ref, out_ref, rt, stage, sem):
    for f in range(16):
        rt[f] = right_ref[f].T

    def put(g):
        return pltpu.make_async_copy(stage.at[g], out_ref.at[:, pos_ref[g]], sem.at[g])

    def one(g, _):
        acc = jnp.zeros((2 * TW, TW), jnp.float32)
        for q in range(8):
            s = src_ref[g, q]
            f = fac_ref[g, q]
            amps = jnp.concatenate([amp_ref[0, s], amp_ref[1, s]], axis=1)
            half = jnp.dot(left_ref[f], amps, preferred_element_type=jnp.float32).astype(
                jnp.bfloat16
            )
            both = jnp.concatenate([half[:, :TW], half[:, TW:]], axis=0)
            acc = acc + jnp.dot(both, rt[f], preferred_element_type=jnp.float32)
        stage[g] = acc.astype(jnp.bfloat16).reshape(J, TW, TW)
        put(g).start()
        return 0

    lax.fori_loop(0, TERMS, one, 0)

    def finish(g, _):
        put(g).wait()
        return 0

    lax.fori_loop(0, TERMS, finish, 0)


def ladder_terms(sources, factors, places, amplitudes, left, right):
    smem = pl.BlockSpec(memory_space=pltpu.SMEM)
    vmem = pl.BlockSpec(memory_space=pltpu.VMEM)
    return pl.pallas_call(
        ladder_kernel,
        out_shape=jax.ShapeDtypeStruct((J, NX * TERMS, TW, TW), jnp.bfloat16),
        in_specs=[smem, smem, smem, vmem, vmem, vmem],
        out_specs=pl.BlockSpec(memory_space=pl.ANY),
        scratch_shapes=[
            pltpu.VMEM((16, TW, TW), jnp.bfloat16),
            pltpu.VMEM((TERMS, J, TW, TW), jnp.bfloat16),
            pltpu.SemaphoreType.DMA((TERMS,)),
        ],
        compiler_params=pltpu.CompilerParams(vmem_limit_bytes=32 * 2**20),
        cost_estimate=pl.CostEstimate(
            flops=2 * 1024 * TW**3, bytes_accessed=4 * 2**20, transcendentals=0
        ),
    )(sources, factors, places, amplitudes, left, right)


def route_kernel(
    first, cap, entries, perm_ref, same_ref, end_ref, some_ref, p_ref, out_ref,
    recv, stage, sums, zs, zr, xs_sem, fs_sem, lx_sem, rx_sem, zs_sem, zr_sem,
):
    t = lax.axis_index("tile")
    y = lax.axis_index("occ")
    core = t % NC
    x = (t // NC) % NX
    z = t // (NC * NX)
    m = t % (NC * NX)

    def at(zz, xx, cc):
        return {"tile": (zz * NX + xx) * NC + cc, "occ": y}

    sibling = at(z, x, 1 - core)
    ups = at((z + 1) % NZ, x, core)
    downs = at((z + NZ - 1) % NZ, x, core)
    barrier = pltpu.get_barrier_semaphore()
    partners = [at(z, (x + d) % NX, core) for d in range(1, NX)] + [sibling, ups, downs]
    for partner in partners:
        pl.semaphore_signal(barrier, inc=1, device_id=partner, device_id_type=MESH)
    pl.semaphore_wait(barrier, len(partners))

    def mine(h, xx):
        return p_ref.at[h // PARTS, xx, pl.ds(first, cap), pl.ds((h % PARTS) * ROWS, ROWS)]

    def send_x(h, d):
        xx = (x + d) % NX
        return pltpu.make_async_remote_copy(
            src_ref=mine(h, xx), dst_ref=recv.at[h, m],
            send_sem=xs_sem.at[h, d], recv_sem=rx_sem.at[h, m],
            device_id=at(z, xx, core), device_id_type=MESH,
        )

    def send_own(h):
        return pltpu.make_async_remote_copy(
            src_ref=mine(h, x), dst_ref=recv.at[h, m],
            send_sem=xs_sem.at[h, 0], recv_sem=rx_sem.at[h, m],
            device_id=sibling, device_id_type=MESH,
        )

    def copy_own(h):
        return pltpu.make_async_copy(mine(h, x), recv.at[h, m], lx_sem.at[h])

    def forward(h, d):
        source = ((x + d) % NX) * NC + core
        return pltpu.make_async_remote_copy(
            src_ref=recv.at[h, source], dst_ref=recv.at[h, source],
            send_sem=fs_sem.at[h, d], recv_sem=rx_sem.at[h, source],
            device_id=sibling, device_id_type=MESH,
        )

    def arrived(h, source):
        return pltpu.make_async_copy(recv.at[h, source], recv.at[h, source], rx_sem.at[h, source])

    def start_x(h):
        for d in range(1, NX):
            send_x(h, d).start()
        send_own(h).start()
        copy_own(h).start()

    def send_z(h, way, step):
        if step == 0:
            part = pl.ds(4 * way, 4)
        else:
            part = pl.ds(0, SLOTS)
        return pltpu.make_async_remote_copy(
            src_ref=zs.at[h, way, step, part], dst_ref=zr.at[h, way, step, part],
            send_sem=zs_sem.at[h, way, step], recv_sem=zr_sem.at[h, way, step],
            device_id=ups if way == 0 else downs, device_id_type=MESH,
        )

    def own(h, zz, s):
        place = zz * SLOTS + s
        value = sums[h % RING, end_ref[place]]
        return jnp.where(some_ref[place] != 0, value, 0.0)

    def z_step(h, step):
        for way in range(2):
            if step > 0:
                send_z(h, way, step - 1).wait_recv()
            zz = (z + 4 - step) % NZ if way == 0 else (z + 4 + step) % NZ
            for s in range(4 * way, 4 * way + 4) if step == 0 else range(SLOTS):
                value = own(h, zz, s)
                if step > 1 or (step == 1 and s // 4 == way):
                    value = value + zr[h, way, step - 1, s].astype(jnp.float32)
                zs[h, way, step, s] = value.astype(jnp.bfloat16)
            send_z(h, way, step).start()

    def finish(h):
        for way in range(2):
            send_z(h, way, 3).wait_recv()
        for s in range(SLOTS):
            total = own(h, z, s) + zr[h, 0, 3, s].astype(jnp.float32)
            total = total + zr[h, 1, 3, s].astype(jnp.float32)
            out_ref[h // PARTS, s, pl.ds((h % PARTS) * ROWS, ROWS)] = total

    def collect(h):
        for d in range(1, NX):
            arrived(h, ((x + d) % NX) * NC + core).wait()
            forward(h, d).start()
        copy_own(h).wait()
        for d in range(NX):
            arrived(h, ((x + d) % NX) * NC + 1 - core).wait()
        for source in range(NX * NC):
            stage[source * cap : (source + 1) * cap] = recv[h, source]

        def entry(e, total):
            value = stage[perm_ref[e]].astype(jnp.float32)
            total = value + jnp.where(same_ref[e] != 0, total, 0.0)
            sums[h % RING, e] = total
            return total

        lax.fori_loop(0, entries, entry, jnp.zeros((ROWS, TW), jnp.float32), unroll=4)

    start_x(0)

    def turn(i, _):
        @pl.when(i + 1 < CHUNKS)
        def _():
            start_x(i + 1)

        @pl.when(i < CHUNKS)
        def _():
            collect(i)
            z_step(i, 0)

        for step in range(1, 4):
            @pl.when((i >= step) & (i - step < CHUNKS))
            def _(step=step):
                z_step(i - step, step)

        @pl.when(i >= 4)
        def _():
            finish(i - 4)

        return 0

    lax.fori_loop(0, CHUNKS + 4, turn, 0)

    def drain(h, _):
        for d in range(1, NX):
            send_x(h, d).wait_send()
            forward(h, d).wait_send()
        send_own(h).wait_send()
        for way in range(2):
            for step in range(4):
                send_z(h, way, step).wait_send()
        return 0

    lax.fori_loop(0, CHUNKS, drain, 0)


def route(first, cap, entries, collective_id, perm, same, end, some, packed):
    smem = pl.BlockSpec(memory_space=pltpu.SMEM)
    dma = pltpu.SemaphoreType.DMA
    return pl.pallas_call(
        functools.partial(route_kernel, first, cap, entries),
        out_shape=jax.ShapeDtypeStruct((J, SLOTS, TW, TW), jnp.float32),
        in_specs=[smem, smem, smem, smem, pl.BlockSpec(memory_space=pl.ANY)],
        out_specs=pl.BlockSpec(memory_space=pltpu.VMEM),
        scratch_shapes=[
            pltpu.VMEM((CHUNKS, NX * NC, cap, ROWS, TW), jnp.bfloat16),
            pltpu.VMEM((NX * NC * cap, ROWS, TW), jnp.bfloat16),
            pltpu.VMEM((RING, entries, ROWS, TW), jnp.float32),
            pltpu.VMEM((CHUNKS, 2, 4, SLOTS, ROWS, TW), jnp.bfloat16),
            pltpu.VMEM((CHUNKS, 2, 4, SLOTS, ROWS, TW), jnp.bfloat16),
            dma((CHUNKS, NX)),
            dma((CHUNKS, NX)),
            dma((CHUNKS,)),
            dma((CHUNKS, NX * NC)),
            dma((CHUNKS, 2, 4)),
            dma((CHUNKS, 2, 4)),
        ],
        compiler_params=pltpu.CompilerParams(
            collective_id=collective_id, has_side_effects=True, vmem_limit_bytes=56 * 2**20
        ),
        cost_estimate=pl.CostEstimate(
            flops=2**22, bytes_accessed=8 * 2**20, transcendentals=0
        ),
    )(perm, same, end, some, packed)


def ranks_in_column(keys):
    column = (keys // (SLOTS * NC)) % NX
    order = jnp.arange(TERMS, dtype=jnp.int32)
    earlier = order[:, None] > order[None, :]
    alike = column[..., :, None] == column[..., None, :]
    return column, jnp.sum((alike & earlier).astype(jnp.int32), axis=-1)


def row_iota(shape, axis):
    return lax.broadcasted_iota(jnp.int32, shape, axis)


def as_column(row):
    diagonal = row_iota((LANES, LANES), 0) == row_iota((LANES, LANES), 1)
    return jnp.sum(jnp.where(diagonal, row, 0), axis=1, keepdims=True)


def main_kernel(
    blocks_ref, owners_ref, slots_ref, src_hbm, fac_hbm, amp_hbm, exch_hbm, left_hbm, right_hbm, ints_hbm,
    out_ref, flag_ref,
    src_ref, fac_ref, keys_v, amp_ref, exch_ref, left_ref, right_ref, ints_ref, rt, terms, packed, recv, stage, sums,
    zs, zr, ysend, yrecv, fsend, frecv, labels_out, labels_in, flags_out, flags_in,
    pack_v, plan_v, pack_s, plan_s, flag_s,
    in_sem, xs_sem, lx_sem, rx_sem, zs_sem, zr_sem, ys_sem, yr_sem, ls_sem, lr_sem,
    gs_sem, gr_sem, sm_sem, es_sem, er_sem,
):
    t = lax.axis_index("tile")
    y = lax.axis_index("occ")
    core = t % NC
    x = (t // NC) % NX
    z = t // (NC * NX)
    m = t % (NC * NX)

    def at(zz, xx, cc):
        return {"tile": (zz * NX + xx) * NC + cc, "occ": y}

    def at_y(d):
        return {"tile": t, "occ": (y + d) % 4}

    def at_m(d):
        return {"tile": z * (NX * NC) + (m + d) % (NX * NC), "occ": y}

    def at_z(d):
        return at((z + d) % NZ, x, core)

    sibling = at(z, x, 1 - core)
    ups = at_z(1)
    downs = at_z(NZ - 1)

    loads = [
        pltpu.make_async_copy(hbm, ref, in_sem.at[n])
        for n, (hbm, ref) in enumerate(
            [(src_hbm, src_ref), (fac_hbm, fac_ref), (right_hbm, right_ref),
             (left_hbm, left_ref), (amp_hbm, amp_ref), (ints_hbm, ints_ref),
             (exch_hbm, exch_ref)]
        )
    ]
    for load in loads[:5]:
        load.start()

    barrier = pltpu.get_barrier_semaphore()
    partners = [at_m(d) for d in range(1, NX * NC)] + [at_z(d) for d in range(1, NZ)]
    partners = partners + [at_y(d) for d in range(1, 4)]
    for partner in partners:
        pl.semaphore_signal(barrier, inc=1, device_id=partner, device_id_type=MESH)

    lane = row_iota((LANES, LANES), 1)
    line = row_iota((LANES, LANES), 0)
    keys_v[...] = jnp.zeros((8, LANES), jnp.int32)
    keys_v[0:1, 0:TERMS] = owners_ref[...] * SLOTS + slots_ref[...]
    keys = keys_v[0:1]
    key_column = as_column(keys)
    real = line < TERMS
    column_row = jnp.where(row_iota((1, LANES), 1) < TERMS, (keys // 16) % NX, NX)
    column = (key_column // 16) % NX
    rank = jnp.sum(
        jnp.where((column_row == column) & (lane < line), 1, 0), axis=1, keepdims=True
    )
    pack_v[...] = jnp.broadcast_to(
        jnp.sum(jnp.where(real & (column * TERMS + rank == lane), line, 0), axis=0, keepdims=True),
        (8, LANES),
    )
    label = ((key_column // 8) % NC) * 64 + (key_column // 64) * SLOTS + key_column % SLOTS
    for xx in range(NX):
        here = real & (column == xx) & (rank < CAP) & (m * 16 + rank == lane)
        row = jnp.sum(jnp.where(here, label + 1, 0), axis=0, keepdims=True)
        labels_out[xx] = jnp.broadcast_to(row, (8, LANES))
    over = jnp.max(jnp.where(real & (rank >= CAP), 1, 0), axis=0, keepdims=True)
    labels_out[NX] = jnp.broadcast_to(over, (8, LANES))
    pack_copy = pltpu.make_async_copy(pack_v, pack_s, sm_sem.at[0])
    pack_copy.start()

    for load in loads[:3]:
        load.wait()
    for f in range(16):
        rt[f] = right_ref[f].T
    for load in loads[3:5]:
        load.wait()
    for load in loads[5:]:
        load.start()


    def one(g, j):
        halves, rights = [], []
        for q in range(8):
            f = fac_ref[q, g]
            half = jnp.dot(
                left_ref[f], amp_ref[j, src_ref[q, g]], preferred_element_type=jnp.float32
            )
            halves.append(half.astype(jnp.bfloat16))
            rights.append(rt[f])
        acc = jnp.dot(
            jnp.concatenate(halves, axis=1), jnp.concatenate(rights, axis=0),
            preferred_element_type=jnp.float32,
        )
        terms[j, g] = acc.astype(jnp.bfloat16)
        return j

    lax.fori_loop(0, TERMS // 2, one, 0, unroll=4)
    pl.semaphore_wait(barrier, len(partners))

    def send_label(d, which):
        if which == 0:
            part = (((m + d) % (NX * NC)) // NC)
        else:
            part = NX
        return pltpu.make_async_remote_copy(
            src_ref=labels_out.at[part], dst_ref=labels_in.at[which, m],
            send_sem=ls_sem.at[which, d], recv_sem=lr_sem.at[which, m],
            device_id=at_m(d), device_id_type=MESH,
        )

    def label_from(d, which):
        source = (m + d) % (NX * NC)
        return pltpu.make_async_copy(
            labels_in.at[which, source], labels_in.at[which, source], lr_sem.at[which, source]
        )

    for d in range(1, NX * NC):
        for which in range(2):
            send_label(d, which).start()
    labels_in[0, m] = labels_out[x]
    labels_in[1, m] = labels_out[NX]

    lax.fori_loop(TERMS // 2, TERMS, one, 0, unroll=4)

    def send_x(h, d, cc):
        to = at(z, (x + d) % NX, cc)
        return pltpu.make_async_remote_copy(
            src_ref=packed.at[h, (x + d) % NX, cc], dst_ref=recv.at[h, m],
            send_sem=xs_sem.at[h, d, cc], recv_sem=rx_sem.at[h, m],
            device_id=to, device_id_type=MESH,
        )

    def send_own(h):
        return pltpu.make_async_remote_copy(
            src_ref=packed.at[h, x, 1 - core], dst_ref=recv.at[h, m],
            send_sem=xs_sem.at[h, 0, 0], recv_sem=rx_sem.at[h, m],
            device_id=sibling, device_id_type=MESH,
        )

    def copy_own(h):
        return pltpu.make_async_copy(packed.at[h, x, core], recv.at[h, m], lx_sem.at[h])

    def arrived(h, source):
        return pltpu.make_async_copy(recv.at[h, source], recv.at[h, source], rx_sem.at[h, source])

    def start_x(h):
        for d in (2, 1, 3, 0):
            xx = (x + d) % NX
            for cc in range(NC):
                rows = pl.ds(cc * (TW // 2) + (h % QUARTERS) * HALF, HALF)
                for k in range(CAP):
                    packed[h, xx, cc, k] = terms[h // QUARTERS, pack_s[0, xx * TERMS + k], rows]
            if d:
                for cc in range(NC):
                    send_x(h, d, cc).start()
        send_own(h).start()
        copy_own(h).start()

    pack_copy.wait()
    start_x(0)
    start_x(1)

    got = labels_out[x, 0:1] * 0
    spill = labels_out[NX, 0:1] * 0
    for d in range(1, NX * NC):
        label_from(d, 0).wait()
        label_from(d, 1).wait()
    for source in range(NX * NC):
        got = got + labels_in[0, source, 0:1]
        spill = spill + labels_in[1, source, 0:1]
    flags_out[...] = jnp.broadcast_to(spill, (8, LANES))

    def send_flag(d):
        return pltpu.make_async_remote_copy(
            src_ref=flags_out, dst_ref=flags_in.at[z],
            send_sem=gs_sem.at[d], recv_sem=gr_sem.at[z],
            device_id=at_z(d), device_id_type=MESH,
        )

    for d in range(1, NZ):
        send_flag(d).start()
    flags_in[z] = jnp.broadcast_to(spill, (8, LANES))

    goal_row = jnp.where(got > 0, got - 1, LANES)
    order_row = goal_row * LANES + row_iota((1, LANES), 1)
    goal = as_column(goal_row)
    order = goal * LANES + row_iota((LANES, 1), 0)
    before = order_row < order
    place = jnp.sum(jnp.where(before, 1, 0), axis=1, keepdims=True)
    follows = jnp.sum(jnp.where(before & (goal_row == goal), 1, 0), axis=1, keepdims=True)
    hit = place == lane
    number = row_iota((LANES, 1), 0)
    spot = (number // 16) * CAP + jnp.minimum(number % 16, CAP - 1)
    perm_row = jnp.sum(jnp.where(hit, spot, 0), axis=0, keepdims=True)
    same_row = jnp.sum(jnp.where(hit, jnp.minimum(follows, 1), 0), axis=0, keepdims=True)
    end_row = jnp.sum(jnp.where(goal <= lane, 1, 0), axis=0, keepdims=True)
    end_row = jnp.minimum(jnp.maximum(end_row - 1, 0), NX * NC * CAP - 1)
    some_row = jnp.sum(jnp.where(goal == lane, 1, 0), axis=0, keepdims=True)
    pick = row_iota((8, LANES), 0)
    plan_v[...] = jnp.where(
        pick == 0, perm_row, jnp.where(pick == 1, same_row, jnp.where(pick == 2, end_row, some_row))
    )
    plan_copy = pltpu.make_async_copy(plan_v, plan_s, sm_sem.at[1])
    plan_copy.start()

    def cycle(s, _):
        rows = jnp.concatenate([amp_ref[0, s], amp_ref[1, s]], axis=1)
        ints = ints_ref[blocks_ref[s]]
        prod = jnp.dot(rows, ints, preferred_element_type=jnp.float32)
        for j in range(8):
            ysend[j, s] = prod[:, j * TW : (j + 1) * TW].astype(jnp.bfloat16)
        return 0

    def send_y(d):
        return pltpu.make_async_remote_copy(
            src_ref=ysend.at[pl.ds(((y + d) % 4) * J, J)], dst_ref=yrecv.at[d],
            send_sem=ys_sem.at[d], recv_sem=yr_sem.at[d],
            device_id=at_y(d), device_id_type=MESH,
        )

    plan_copy.wait()

    def send_z(h, way, step, half):
        part = pl.ds(SLOTS * half, SLOTS)
        return pltpu.make_async_remote_copy(
            src_ref=zs.at[h, way, step, part], dst_ref=zr.at[h, way, step, part],
            send_sem=zs_sem.at[h, way, step, half], recv_sem=zr_sem.at[h, way, step, half],
            device_id=ups if way == 0 else downs, device_id_type=MESH,
        )

    def own(h, zz, n):
        goal = (n // SLOTS) * 64 + zz * SLOTS + n % SLOTS
        value = sums[h, plan_s[2, goal]]
        return jnp.where(plan_s[3, goal] != 0, value, 0.0)

    def z_step(h, step, far):
        for way in range(2):
            half = way if far else 1 - way
            first = step == (0 if far else 1)
            if not first:
                send_z(h, way, step - 1, half).wait_recv()
            zz = (z + 4 - step) % NZ if way == 0 else (z + 4 + step) % NZ
            for n in range(SLOTS * half, SLOTS * half + SLOTS):
                value = own(h, zz, n)
                if not first:
                    value = value + zr[h, way, step - 1, n].astype(jnp.float32)
                zs[h, way, step, n] = value.astype(jnp.bfloat16)
            send_z(h, way, step, half).start()

    def send_end(h):
        return pltpu.make_async_remote_copy(
            src_ref=fsend.at[h], dst_ref=frecv.at[h], send_sem=es_sem.at[h],
            recv_sem=er_sem.at[h], device_id=sibling, device_id_type=MESH,
        )

    def finish(h):
        for way in range(2):
            for half in range(2):
                send_z(h, way, 3, half).wait_recv()

        def total(cc, s):
            n = cc * SLOTS + s
            value = own(h, z, n) + zr[h, 0, 3, n].astype(jnp.float32)
            return value + zr[h, 1, 3, n].astype(jnp.float32)

        for s in range(SLOTS):
            fsend[h, s] = total(1 - core, s)
        send_end(h).start()
        rows = pl.ds(core * (TW // 2) + (h % QUARTERS) * HALF, HALF)
        for s in range(SLOTS):
            out_ref[h // QUARTERS, s, rows] = total(core, s)

    def collect(h):
        copy_own(h).wait()
        for d in range(1, NX * NC):
            arrived(h, (m + d) % (NX * NC)).wait()
        for source in range(NX * NC):
            stage[source * CAP : (source + 1) * CAP] = recv[h, source]

        def entry(e, total):
            value = stage[plan_s[0, e]].astype(jnp.float32)
            total = value + jnp.where(plan_s[1, e] != 0, total, 0.0)
            sums[h, e] = total
            return total

        lax.fori_loop(0, NX * NC * CAP, entry, jnp.zeros((HALF, TW), jnp.float32), unroll=8)

    def drain_x(h):
        for d in range(1, NX):
            for cc in range(NC):
                send_x(h, d, cc).wait_send()
        send_own(h).wait_send()

    def drain_z(h):
        send_end(h).wait_send()
        for way in range(2):
            for step in range(4):
                for half in range(2):
                    if step or half == way:
                        send_z(h, way, step, half).wait_send()

    def turn(i, _):
        @pl.when(i < 2)
        def _():
            lax.fori_loop(0, TERMS // 2, lambda g, j: one(i * (TERMS // 2) + g, j), 1, unroll=4)

        @pl.when(i + 2 < STEPS)
        def _():
            start_x(i + 2)

        @pl.when(i < STEPS)
        def _():
            collect(i)
            z_step(i, 0, True)
            z_step(i, 1, False)

        for step in range(1, 4):
            @pl.when((i >= step) & (i - step < STEPS))
            def _(step=step):
                z_step(i - step, step, True)
                if step < 3:
                    z_step(i - step, step + 1, False)

        @pl.when((i >= 1) & (i < 5))
        def _():
            @pl.when(i == 1)
            def _():
                loads[5].wait()

            lax.fori_loop(i * 2 - 2, i * 2, cycle, 0)

            @pl.when(i == 4)
            def _():
                for d in range(1, 4):
                    send_y(d).start()

        @pl.when((i >= 2) & (i - 2 < STEPS))
        def _():
            drain_x(i - 2)

        @pl.when(i >= 5)
        def _():
            drain_z(i - 5)

        @pl.when(i >= 4)
        def _():
            finish(i - 4)

        return 0

    lax.fori_loop(0, STEPS + 4, turn, 0)

    def ending(h, _):
        send_end(h).wait_recv()
        rows = pl.ds((1 - core) * (TW // 2) + (h % QUARTERS) * HALF, HALF)
        for s in range(SLOTS):
            out_ref[h // QUARTERS, s, rows] = frecv[h, s]
        return 0

    lax.fori_loop(0, STEPS, ending, 0)

    loads[6].wait()
    for d in range(1, 4):
        send_y(d).wait_recv()

    def add(s, _):
        for j in range(J):
            total = out_ref[j, s] + exch_ref[j, s].astype(jnp.float32)
            total = total + ysend[y * J + j, s].astype(jnp.float32)
            for d in range(1, 4):
                total = total + yrecv[d, j, s].astype(jnp.float32)
            out_ref[j, s] = total
        return 0

    lax.fori_loop(0, SLOTS, add, 0)

    flags = flags_in[z]
    for d in range(1, NZ):
        source = (z + d) % NZ
        pltpu.make_async_copy(flags_in.at[source], flags_in.at[source], gr_sem.at[source]).wait()
        flags = flags + flags_in[source]
    pack_v[...] = jnp.broadcast_to(jnp.max(flags, axis=1, keepdims=True), (8, LANES))
    flag_copy = pltpu.make_async_copy(pack_v, flag_s, sm_sem.at[2])
    flag_copy.start()

    for d in range(1, NX * NC):
        for which in range(2):
            send_label(d, which).wait_send()
    for d in range(1, NZ):
        send_flag(d).wait_send()
    for d in range(1, 4):
        send_y(d).wait_send()

    drain_z(STEPS - 1)
    flag_copy.wait()
    flag_ref[0] = flag_s[0, 0]


def main_call(sources, factors, blocks, owners, slots, amplitudes, exchange, left, right, ints):
    smem = pl.BlockSpec(memory_space=pltpu.SMEM)
    vmem = pl.BlockSpec(memory_space=pltpu.VMEM)
    hbm = pl.BlockSpec(memory_space=pl.ANY)
    dma = pltpu.SemaphoreType.DMA
    entries = NX * NC * CAP
    block = (J, SLOTS, TW, TW)
    return pl.pallas_call(
        main_kernel,
        out_shape=[
            jax.ShapeDtypeStruct(block, jnp.float32),
            jax.ShapeDtypeStruct((1,), jnp.int32),
        ],
        in_specs=[smem, vmem, vmem] + [hbm] * 7,
        out_specs=[vmem, smem],
        scratch_shapes=[
            pltpu.SMEM((8, TERMS), jnp.int32),
            pltpu.SMEM((8, TERMS), jnp.int32),
            pltpu.VMEM((8, LANES), jnp.int32),
            pltpu.VMEM(block, jnp.bfloat16),
            pltpu.VMEM(block, jnp.bfloat16),
            pltpu.VMEM((16, TW, TW), jnp.bfloat16),
            pltpu.VMEM((16, TW, TW), jnp.bfloat16),
            pltpu.VMEM((2, 2 * TW, 8 * TW), jnp.bfloat16),
            pltpu.VMEM((16, TW, TW), jnp.bfloat16),
            pltpu.VMEM((J, TERMS, TW, TW), jnp.bfloat16),
            pltpu.VMEM((STEPS, NX, NC, CAP, HALF, TW), jnp.bfloat16),
            pltpu.VMEM((STEPS, NX * NC, CAP, HALF, TW), jnp.bfloat16),
            pltpu.VMEM((entries, HALF, TW), jnp.bfloat16),
            pltpu.VMEM((STEPS, entries, HALF, TW), jnp.float32),
            pltpu.VMEM((STEPS, 2, 4, GOALS, HALF, TW), jnp.bfloat16),
            pltpu.VMEM((STEPS, 2, 4, GOALS, HALF, TW), jnp.bfloat16),
            pltpu.VMEM((8, SLOTS, TW, TW), jnp.bfloat16),
            pltpu.VMEM((4,) + block, jnp.bfloat16),
            pltpu.VMEM((STEPS, SLOTS, HALF, TW), jnp.float32),
            pltpu.VMEM((STEPS, SLOTS, HALF, TW), jnp.float32),
            pltpu.VMEM((NX + 1, 8, LANES), jnp.int32),
            pltpu.VMEM((2, NX * NC, 8, LANES), jnp.int32),
            pltpu.VMEM((8, LANES), jnp.int32),
            pltpu.VMEM((NZ, 8, LANES), jnp.int32),
            pltpu.VMEM((8, LANES), jnp.int32),
            pltpu.VMEM((8, LANES), jnp.int32),
            pltpu.SMEM((8, LANES), jnp.int32),
            pltpu.SMEM((8, LANES), jnp.int32),
            pltpu.SMEM((8, LANES), jnp.int32),
            dma((7,)),
            dma((STEPS, NX, NC)),
            dma((STEPS,)),
            dma((STEPS, NX * NC)),
            dma((STEPS, 2, 4, 2)),
            dma((STEPS, 2, 4, 2)),
            dma((4,)),
            dma((4,)),
            dma((2, NX * NC)),
            dma((2, NX * NC)),
            dma((NZ,)),
            dma((NZ,)),
            dma((3,)),
            dma((STEPS,)),
            dma((STEPS,)),
        ],
        compiler_params=pltpu.CompilerParams(
            collective_id=0, has_side_effects=True, vmem_limit_bytes=58 * 2**20
        ),
        cost_estimate=pl.CostEstimate(
            flops=2 * 1024 * TW**3, bytes_accessed=8 * 2**20, transcendentals=0
        ),
    )(blocks, owners, slots, sources, factors, amplitudes, exchange, left, right, ints)


def spilled(
    amplitudes, left_factors, right_factors, ladder_sources, ladder_factors, keys
):
    tile = lax.axis_index("tile")
    table = lax.all_gather(keys, "tile", axis=0)
    column, rank = ranks_in_column(keys)
    packed = ladder_terms(
        ladder_sources, ladder_factors, column * TERMS + rank, amplitudes, left_factors,
        right_factors,
    ).reshape(J, NX, TERMS, TW, TW)
    width = TERMS - CAP
    all_ranks = ranks_in_column(table)[1]
    group = (tile // 8) * 8
    here = lax.dynamic_slice_in_dim(table, group, 8, 0).reshape(-1)
    here_rank = lax.dynamic_slice_in_dim(all_ranks, group, 8, 0).reshape(-1)
    number = jnp.arange(8 * TERMS, dtype=jnp.int32)
    valid = ((here // SLOTS) % 8 == tile % 8) & (here_rank >= CAP)
    target = jnp.where(valid, (here // (SLOTS * 8)) * SLOTS + here % SLOTS, 64)
    order = target * 256 + number
    place = jnp.sum((order[None, :] < order[:, None]).astype(jnp.int32), axis=1)
    hit = place[None, :] == number[:, None]
    spot = (number // TERMS) * width + jnp.maximum(here_rank - CAP, 0)
    perm = jnp.sum(jnp.where(hit, spot[None, :], 0), axis=1)
    sorted_target = jnp.sum(jnp.where(hit, target[None, :], 0), axis=1)
    same = jnp.concatenate(
        [jnp.zeros((1,), jnp.int32), (sorted_target[1:] == sorted_target[:-1]).astype(jnp.int32)]
    )
    goal = jnp.arange(64, dtype=jnp.int32)[:, None]
    end = jnp.maximum(jnp.sum((target[None, :] <= goal).astype(jnp.int32), axis=1) - 1, 0)
    some = jnp.sum((target[None, :] == goal).astype(jnp.int32), axis=1)
    entries = 8 * width
    return route(CAP, width, entries, 1, perm[:entries], same[:entries], end, some, packed)


def local(
    amplitudes, exchange_ints, left_factors, right_factors, ladder_sources, ladder_factors,
    dest_owners, dest_slots, cycle_blocks, cycle_ints,
):
    total, flags = main_call(
        ladder_sources.T, ladder_factors.T, cycle_blocks, dest_owners.reshape(1, TERMS),
        dest_slots[None, :], amplitudes, exchange_ints,
        left_factors, right_factors, cycle_ints,
    )

    def whole():
        return total.astype(jnp.bfloat16)

    def more():
        keys = dest_owners[:, 0] * SLOTS + dest_slots
        rest = spilled(
            amplitudes, left_factors, right_factors, ladder_sources, ladder_factors, keys
        )
        return (total + rest).astype(jnp.bfloat16)

    return lax.cond(flags[0] > 0, more, whole)


def solution(mesh):
    placed = (
        P("occ", "tile", None, None),
        P("occ", "tile", None, None),
        P("tile", None, None),
        P("tile", None, None),
        P("tile", None),
        P("tile", None),
        P("tile", None),
        P("tile"),
        P("tile"),
        P("tile", "occ", None),
    )
    return jax.shard_map(
        local, mesh=mesh, in_specs=placed, out_specs=P("occ", "tile", None, None), check_vma=False
    )
```

```python
import functools

import jax
import jax.numpy as jnp
from jax import lax
from jax.experimental import pallas as pl
from jax.experimental.pallas import tpu as pltpu
from jax.sharding import PartitionSpec as P

MESH = pl.DeviceIdType.MESH
NZ, NX, NC = 8, 4, 2
TERMS = 32
SLOTS = 8
TW = 128
J = 2
ROWS = 32
PARTS = TW // ROWS
CHUNKS = J * PARTS
RING = 5
CAP = 14
LANES = 128
HALF = 16
QUARTERS = TW // 2 // HALF
STEPS = J * QUARTERS
GOALS = NC * SLOTS


def ladder_kernel(src_ref, fac_ref, pos_ref, amp_ref, left_ref, right_ref, out_ref, rt, stage, sem):
    for f in range(16):
        rt[f] = right_ref[f].T

    def put(g):
        return pltpu.make_async_copy(stage.at[g], out_ref.at[:, pos_ref[g]], sem.at[g])

    def one(g, _):
        acc = jnp.zeros((2 * TW, TW), jnp.float32)
        for q in range(8):
            s = src_ref[g, q]
            f = fac_ref[g, q]
            amps = jnp.concatenate([amp_ref[0, s], amp_ref[1, s]], axis=1)
            half = jnp.dot(left_ref[f], amps, preferred_element_type=jnp.float32).astype(
                jnp.bfloat16
            )
            both = jnp.concatenate([half[:, :TW], half[:, TW:]], axis=0)
            acc = acc + jnp.dot(both, rt[f], preferred_element_type=jnp.float32)
        stage[g] = acc.astype(jnp.bfloat16).reshape(J, TW, TW)
        put(g).start()
        return 0

    lax.fori_loop(0, TERMS, one, 0)

    def finish(g, _):
        put(g).wait()
        return 0

    lax.fori_loop(0, TERMS, finish, 0)


def ladder_terms(sources, factors, places, amplitudes, left, right):
    smem = pl.BlockSpec(memory_space=pltpu.SMEM)
    vmem = pl.BlockSpec(memory_space=pltpu.VMEM)
    return pl.pallas_call(
        ladder_kernel,
        out_shape=jax.ShapeDtypeStruct((J, NX * TERMS, TW, TW), jnp.bfloat16),
        in_specs=[smem, smem, smem, vmem, vmem, vmem],
        out_specs=pl.BlockSpec(memory_space=pl.ANY),
        scratch_shapes=[
            pltpu.VMEM((16, TW, TW), jnp.bfloat16),
            pltpu.VMEM((TERMS, J, TW, TW), jnp.bfloat16),
            pltpu.SemaphoreType.DMA((TERMS,)),
        ],
        compiler_params=pltpu.CompilerParams(vmem_limit_bytes=32 * 2**20),
        cost_estimate=pl.CostEstimate(
            flops=2 * 1024 * TW**3, bytes_accessed=4 * 2**20, transcendentals=0
        ),
    )(sources, factors, places, amplitudes, left, right)


def route_kernel(
    first, cap, entries, perm_ref, same_ref, end_ref, some_ref, p_ref, out_ref,
    recv, stage, sums, zs, zr, xs_sem, fs_sem, lx_sem, rx_sem, zs_sem, zr_sem,
):
    t = lax.axis_index("tile")
    y = lax.axis_index("occ")
    core = t % NC
    x = (t // NC) % NX
    z = t // (NC * NX)
    m = t % (NC * NX)

    def at(zz, xx, cc):
        return {"tile": (zz * NX + xx) * NC + cc, "occ": y}

    sibling = at(z, x, 1 - core)
    ups = at((z + 1) % NZ, x, core)
    downs = at((z + NZ - 1) % NZ, x, core)
    barrier = pltpu.get_barrier_semaphore()
    partners = [at(z, (x + d) % NX, core) for d in range(1, NX)] + [sibling, ups, downs]
    for partner in partners:
        pl.semaphore_signal(barrier, inc=1, device_id=partner, device_id_type=MESH)
    pl.semaphore_wait(barrier, len(partners))

    def mine(h, xx):
        return p_ref.at[h // PARTS, xx, pl.ds(first, cap), pl.ds((h % PARTS) * ROWS, ROWS)]

    def send_x(h, d):
        xx = (x + d) % NX
        return pltpu.make_async_remote_copy(
            src_ref=mine(h, xx), dst_ref=recv.at[h, m],
            send_sem=xs_sem.at[h, d], recv_sem=rx_sem.at[h, m],
            device_id=at(z, xx, core), device_id_type=MESH,
        )

    def send_own(h):
        return pltpu.make_async_remote_copy(
            src_ref=mine(h, x), dst_ref=recv.at[h, m],
            send_sem=xs_sem.at[h, 0], recv_sem=rx_sem.at[h, m],
            device_id=sibling, device_id_type=MESH,
        )

    def copy_own(h):
        return pltpu.make_async_copy(mine(h, x), recv.at[h, m], lx_sem.at[h])

    def forward(h, d):
        source = ((x + d) % NX) * NC + core
        return pltpu.make_async_remote_copy(
            src_ref=recv.at[h, source], dst_ref=recv.at[h, source],
            send_sem=fs_sem.at[h, d], recv_sem=rx_sem.at[h, source],
            device_id=sibling, device_id_type=MESH,
        )

    def arrived(h, source):
        return pltpu.make_async_copy(recv.at[h, source], recv.at[h, source], rx_sem.at[h, source])

    def start_x(h):
        for d in range(1, NX):
            send_x(h, d).start()
        send_own(h).start()
        copy_own(h).start()

    def send_z(h, way, step):
        if step == 0:
            part = pl.ds(4 * way, 4)
        else:
            part = pl.ds(0, SLOTS)
        return pltpu.make_async_remote_copy(
            src_ref=zs.at[h, way, step, part], dst_ref=zr.at[h, way, step, part],
            send_sem=zs_sem.at[h, way, step], recv_sem=zr_sem.at[h, way, step],
            device_id=ups if way == 0 else downs, device_id_type=MESH,
        )

    def own(h, zz, s):
        place = zz * SLOTS + s
        value = sums[h % RING, end_ref[place]]
        return jnp.where(some_ref[place] != 0, value, 0.0)

    def z_step(h, step):
        for way in range(2):
            if step > 0:
                send_z(h, way, step - 1).wait_recv()
            zz = (z + 4 - step) % NZ if way == 0 else (z + 4 + step) % NZ
            for s in range(4 * way, 4 * way + 4) if step == 0 else range(SLOTS):
                value = own(h, zz, s)
                if step > 1 or (step == 1 and s // 4 == way):
                    value = value + zr[h, way, step - 1, s].astype(jnp.float32)
                zs[h, way, step, s] = value.astype(jnp.bfloat16)
            send_z(h, way, step).start()

    def finish(h):
        for way in range(2):
            send_z(h, way, 3).wait_recv()
        for s in range(SLOTS):
            total = own(h, z, s) + zr[h, 0, 3, s].astype(jnp.float32)
            total = total + zr[h, 1, 3, s].astype(jnp.float32)
            out_ref[h // PARTS, s, pl.ds((h % PARTS) * ROWS, ROWS)] = total

    def collect(h):
        for d in range(1, NX):
            arrived(h, ((x + d) % NX) * NC + core).wait()
            forward(h, d).start()
        copy_own(h).wait()
        for d in range(NX):
            arrived(h, ((x + d) % NX) * NC + 1 - core).wait()
        for source in range(NX * NC):
            stage[source * cap : (source + 1) * cap] = recv[h, source]

        def entry(e, total):
            value = stage[perm_ref[e]].astype(jnp.float32)
            total = value + jnp.where(same_ref[e] != 0, total, 0.0)
            sums[h % RING, e] = total
            return total

        lax.fori_loop(0, entries, entry, jnp.zeros((ROWS, TW), jnp.float32), unroll=4)

    start_x(0)

    def turn(i, _):
        @pl.when(i + 1 < CHUNKS)
        def _():
            start_x(i + 1)

        @pl.when(i < CHUNKS)
        def _():
            collect(i)
            z_step(i, 0)

        for step in range(1, 4):
            @pl.when((i >= step) & (i - step < CHUNKS))
            def _(step=step):
                z_step(i - step, step)

        @pl.when(i >= 4)
        def _():
            finish(i - 4)

        return 0

    lax.fori_loop(0, CHUNKS + 4, turn, 0)

    def drain(h, _):
        for d in range(1, NX):
            send_x(h, d).wait_send()
            forward(h, d).wait_send()
        send_own(h).wait_send()
        for way in range(2):
            for step in range(4):
                send_z(h, way, step).wait_send()
        return 0

    lax.fori_loop(0, CHUNKS, drain, 0)


def route(first, cap, entries, collective_id, perm, same, end, some, packed):
    smem = pl.BlockSpec(memory_space=pltpu.SMEM)
    dma = pltpu.SemaphoreType.DMA
    return pl.pallas_call(
        functools.partial(route_kernel, first, cap, entries),
        out_shape=jax.ShapeDtypeStruct((J, SLOTS, TW, TW), jnp.float32),
        in_specs=[smem, smem, smem, smem, pl.BlockSpec(memory_space=pl.ANY)],
        out_specs=pl.BlockSpec(memory_space=pltpu.VMEM),
        scratch_shapes=[
            pltpu.VMEM((CHUNKS, NX * NC, cap, ROWS, TW), jnp.bfloat16),
            pltpu.VMEM((NX * NC * cap, ROWS, TW), jnp.bfloat16),
            pltpu.VMEM((RING, entries, ROWS, TW), jnp.float32),
            pltpu.VMEM((CHUNKS, 2, 4, SLOTS, ROWS, TW), jnp.bfloat16),
            pltpu.VMEM((CHUNKS, 2, 4, SLOTS, ROWS, TW), jnp.bfloat16),
            dma((CHUNKS, NX)),
            dma((CHUNKS, NX)),
            dma((CHUNKS,)),
            dma((CHUNKS, NX * NC)),
            dma((CHUNKS, 2, 4)),
            dma((CHUNKS, 2, 4)),
        ],
        compiler_params=pltpu.CompilerParams(
            collective_id=collective_id, has_side_effects=True, vmem_limit_bytes=56 * 2**20
        ),
        cost_estimate=pl.CostEstimate(
            flops=2**22, bytes_accessed=8 * 2**20, transcendentals=0
        ),
    )(perm, same, end, some, packed)


def ranks_in_column(keys):
    column = (keys // (SLOTS * NC)) % NX
    order = jnp.arange(TERMS, dtype=jnp.int32)
    earlier = order[:, None] > order[None, :]
    alike = column[..., :, None] == column[..., None, :]
    return column, jnp.sum((alike & earlier).astype(jnp.int32), axis=-1)


def row_iota(shape, axis):
    return lax.broadcasted_iota(jnp.int32, shape, axis)


def as_column(row):
    diagonal = row_iota((LANES, LANES), 0) == row_iota((LANES, LANES), 1)
    return jnp.sum(jnp.where(diagonal, row, 0), axis=1, keepdims=True)


def main_kernel(
    blocks_ref, owners_ref, slots_ref, src_hbm, fac_hbm, amp_hbm, exch_hbm, left_hbm, right_hbm, ints_hbm,
    out_ref, flag_ref,
    src_ref, fac_ref, keys_v, amp_ref, exch_ref, left_ref, right_ref, ints_ref, rt, terms, packed, recv, stage, sums,
    zs, zr, ysend, yrecv, fsend, frecv, labels_out, labels_in, flags_out, flags_in,
    pack_v, plan_v, pack_s, plan_s, flag_s,
    in_sem, xs_sem, lx_sem, rx_sem, zs_sem, zr_sem, ys_sem, yr_sem, ls_sem, lr_sem,
    gs_sem, gr_sem, sm_sem, es_sem, er_sem,
):
    t = lax.axis_index("tile")
    y = lax.axis_index("occ")
    core = t % NC
    x = (t // NC) % NX
    z = t // (NC * NX)
    m = t % (NC * NX)

    def at(zz, xx, cc):
        return {"tile": (zz * NX + xx) * NC + cc, "occ": y}

    def at_y(d):
        return {"tile": t, "occ": (y + d) % 4}

    def at_m(d):
        return {"tile": z * (NX * NC) + (m + d) % (NX * NC), "occ": y}

    def at_z(d):
        return at((z + d) % NZ, x, core)

    sibling = at(z, x, 1 - core)
    ups = at_z(1)
    downs = at_z(NZ - 1)

    loads = [
        pltpu.make_async_copy(hbm, ref, in_sem.at[n])
        for n, (hbm, ref) in enumerate(
            [(src_hbm, src_ref), (fac_hbm, fac_ref), (right_hbm, right_ref),
             (left_hbm, left_ref), (amp_hbm, amp_ref), (ints_hbm, ints_ref),
             (exch_hbm, exch_ref)]
        )
    ]
    for load in loads[:5]:
        load.start()

    barrier = pltpu.get_barrier_semaphore()
    partners = [at_m(d) for d in range(1, NX * NC)] + [at_z(d) for d in range(1, NZ)]
    partners = partners + [at_y(d) for d in range(1, 4)]
    for partner in partners:
        pl.semaphore_signal(barrier, inc=1, device_id=partner, device_id_type=MESH)

    lane = row_iota((LANES, LANES), 1)
    line = row_iota((LANES, LANES), 0)
    keys_v[...] = jnp.zeros((8, LANES), jnp.int32)
    keys_v[0:1, 0:TERMS] = owners_ref[...] * SLOTS + slots_ref[...]
    keys = keys_v[0:1]
    key_column = as_column(keys)
    real = line < TERMS
    column_row = jnp.where(row_iota((1, LANES), 1) < TERMS, (keys // 16) % NX, NX)
    column = (key_column // 16) % NX
    rank = jnp.sum(
        jnp.where((column_row == column) & (lane < line), 1, 0), axis=1, keepdims=True
    )
    pack_v[...] = jnp.broadcast_to(
        jnp.sum(jnp.where(real & (column * TERMS + rank == lane), line, 0), axis=0, keepdims=True),
        (8, LANES),
    )
    label = ((key_column // 8) % NC) * 64 + (key_column // 64) * SLOTS + key_column % SLOTS
    over = jnp.max(jnp.where(real & (rank >= CAP), 1, 0), axis=0, keepdims=True)
    top = row_iota((8, LANES), 0) == 0
    for xx in range(NX):
        here = real & (column == xx) & (rank < CAP) & (m * 16 + rank == lane)
        row = jnp.sum(jnp.where(here, label + 1, 0), axis=0, keepdims=True)
        labels_out[xx] = jnp.where(top, row, over)
    pack_copy = pltpu.make_async_copy(pack_v, pack_s, sm_sem.at[0])
    pack_copy.start()

    for load in loads[:3]:
        load.wait()
    for f in range(16):
        rt[f] = right_ref[f].T
    for load in loads[3:5]:
        load.wait()
    for load in loads[5:]:
        load.start()


    def one(g, j):
        halves, rights = [], []
        for q in range(8):
            f = fac_ref[q, g]
            half = jnp.dot(
                left_ref[f], amp_ref[j, src_ref[q, g]], preferred_element_type=jnp.float32
            )
            halves.append(half.astype(jnp.bfloat16))
            rights.append(rt[f])
        acc = jnp.dot(
            jnp.concatenate(halves, axis=1), jnp.concatenate(rights, axis=0),
            preferred_element_type=jnp.float32,
        )
        terms[j, g] = acc.astype(jnp.bfloat16)
        return j

    lax.fori_loop(0, TERMS // 2, one, 0, unroll=4)
    pl.semaphore_wait(barrier, len(partners))

    def send_label(d):
        return pltpu.make_async_remote_copy(
            src_ref=labels_out.at[((m + d) % (NX * NC)) // NC], dst_ref=labels_in.at[m],
            send_sem=ls_sem.at[d], recv_sem=lr_sem.at[m],
            device_id=at_m(d), device_id_type=MESH,
        )

    def label_from(d):
        source = (m + d) % (NX * NC)
        return pltpu.make_async_copy(
            labels_in.at[source], labels_in.at[source], lr_sem.at[source]
        )

    for d in range(1, NX * NC):
        send_label(d).start()
    labels_in[m] = labels_out[x]

    lax.fori_loop(TERMS // 2, TERMS, one, 0, unroll=4)

    def send_x(h, d, cc):
        to = at(z, (x + d) % NX, cc)
        return pltpu.make_async_remote_copy(
            src_ref=packed.at[h, (x + d) % NX, cc], dst_ref=recv.at[h, m],
            send_sem=xs_sem.at[h, d, cc], recv_sem=rx_sem.at[h, m],
            device_id=to, device_id_type=MESH,
        )

    def send_own(h):
        return pltpu.make_async_remote_copy(
            src_ref=packed.at[h, x, 1 - core], dst_ref=recv.at[h, m],
            send_sem=xs_sem.at[h, 0, 0], recv_sem=rx_sem.at[h, m],
            device_id=sibling, device_id_type=MESH,
        )

    def copy_own(h):
        return pltpu.make_async_copy(packed.at[h, x, core], recv.at[h, m], lx_sem.at[h])

    def arrived(h, source):
        return pltpu.make_async_copy(recv.at[h, source], recv.at[h, source], rx_sem.at[h, source])

    def start_x(h):
        for d in (2, 1, 3, 0):
            xx = (x + d) % NX
            for cc in range(NC):
                rows = pl.ds(cc * (TW // 2) + (h % QUARTERS) * HALF, HALF)
                for k in range(CAP):
                    packed[h, xx, cc, k] = terms[h // QUARTERS, pack_s[0, xx * TERMS + k], rows]
            if d:
                for cc in range(NC):
                    send_x(h, d, cc).start()
        send_own(h).start()
        copy_own(h).start()

    pack_copy.wait()
    start_x(0)
    start_x(1)

    got = labels_out[x, 0:1] * 0
    spill = labels_out[x, 1:2] * 0
    for d in range(1, NX * NC):
        label_from(d).wait()
    for source in range(NX * NC):
        got = got + labels_in[source, 0:1]
        spill = spill + labels_in[source, 1:2]
    flags_out[...] = jnp.broadcast_to(spill, (8, LANES))

    def send_flag(d):
        return pltpu.make_async_remote_copy(
            src_ref=flags_out, dst_ref=flags_in.at[z],
            send_sem=gs_sem.at[d], recv_sem=gr_sem.at[z],
            device_id=at_z(d), device_id_type=MESH,
        )

    for d in range(1, NZ):
        send_flag(d).start()
    flags_in[z] = jnp.broadcast_to(spill, (8, LANES))

    goal_row = jnp.where(got > 0, got - 1, LANES)
    order_row = goal_row * LANES + row_iota((1, LANES), 1)
    goal = as_column(goal_row)
    order = goal * LANES + row_iota((LANES, 1), 0)
    before = order_row < order
    place = jnp.sum(jnp.where(before, 1, 0), axis=1, keepdims=True)
    follows = jnp.sum(jnp.where(before & (goal_row == goal), 1, 0), axis=1, keepdims=True)
    hit = place == lane
    number = row_iota((LANES, 1), 0)
    spot = (number // 16) * CAP + jnp.minimum(number % 16, CAP - 1)
    perm_row = jnp.sum(jnp.where(hit, spot, 0), axis=0, keepdims=True)
    same_row = jnp.sum(jnp.where(hit, jnp.minimum(follows, 1), 0), axis=0, keepdims=True)
    end_row = jnp.sum(jnp.where(goal <= lane, 1, 0), axis=0, keepdims=True)
    end_row = jnp.minimum(jnp.maximum(end_row - 1, 0), NX * NC * CAP - 1)
    some_row = jnp.sum(jnp.where(goal == lane, 1, 0), axis=0, keepdims=True)
    pick = row_iota((8, LANES), 0)
    plan_v[...] = jnp.where(
        pick == 0, perm_row, jnp.where(pick == 1, same_row, jnp.where(pick == 2, end_row, some_row))
    )
    plan_copy = pltpu.make_async_copy(plan_v, plan_s, sm_sem.at[1])
    plan_copy.start()

    def cycle(s, _):
        rows = jnp.concatenate([amp_ref[0, s], amp_ref[1, s]], axis=1)
        ints = ints_ref[blocks_ref[s]]
        prod = jnp.dot(rows, ints, preferred_element_type=jnp.float32)
        for j in range(8):
            ysend[j, s] = prod[:, j * TW : (j + 1) * TW].astype(jnp.bfloat16)
        return 0

    def send_y(d):
        return pltpu.make_async_remote_copy(
            src_ref=ysend.at[pl.ds(((y + d) % 4) * J, J)], dst_ref=yrecv.at[d],
            send_sem=ys_sem.at[d], recv_sem=yr_sem.at[d],
            device_id=at_y(d), device_id_type=MESH,
        )

    plan_copy.wait()

    def send_z(h, way, step, half):
        part = pl.ds(SLOTS * half, SLOTS)
        return pltpu.make_async_remote_copy(
            src_ref=zs.at[h, way, step, part], dst_ref=zr.at[h, way, step, part],
            send_sem=zs_sem.at[h, way, step, half], recv_sem=zr_sem.at[h, way, step, half],
            device_id=ups if way == 0 else downs, device_id_type=MESH,
        )

    def own(h, zz, n):
        goal = (n // SLOTS) * 64 + zz * SLOTS + n % SLOTS
        value = sums[h, plan_s[2, goal]]
        return jnp.where(plan_s[3, goal] != 0, value, 0.0)

    def z_step(h, step, far):
        for way in range(2):
            half = way if far else 1 - way
            first = step == (0 if far else 1)
            if not first:
                send_z(h, way, step - 1, half).wait_recv()
            zz = (z + 4 - step) % NZ if way == 0 else (z + 4 + step) % NZ
            for n in range(SLOTS * half, SLOTS * half + SLOTS):
                value = own(h, zz, n)
                if not first:
                    value = value + zr[h, way, step - 1, n].astype(jnp.float32)
                zs[h, way, step, n] = value.astype(jnp.bfloat16)
            send_z(h, way, step, half).start()

    def send_end(h):
        return pltpu.make_async_remote_copy(
            src_ref=fsend.at[h], dst_ref=frecv.at[h], send_sem=es_sem.at[h],
            recv_sem=er_sem.at[h], device_id=sibling, device_id_type=MESH,
        )

    def finish(h):
        for way in range(2):
            for half in range(2):
                send_z(h, way, 3, half).wait_recv()

        def total(cc, s):
            n = cc * SLOTS + s
            value = own(h, z, n) + zr[h, 0, 3, n].astype(jnp.float32)
            return value + zr[h, 1, 3, n].astype(jnp.float32)

        for s in range(SLOTS):
            fsend[h, s] = total(1 - core, s)
        send_end(h).start()
        rows = pl.ds(core * (TW // 2) + (h % QUARTERS) * HALF, HALF)
        for s in range(SLOTS):
            out_ref[h // QUARTERS, s, rows] = total(core, s)

    def collect(h):
        copy_own(h).wait()
        for d in range(1, NX * NC):
            arrived(h, (m + d) % (NX * NC)).wait()
        for source in range(NX * NC):
            stage[source * CAP : (source + 1) * CAP] = recv[h, source]

        def entry(e, total):
            value = stage[plan_s[0, e]].astype(jnp.float32)
            total = value + jnp.where(plan_s[1, e] != 0, total, 0.0)
            sums[h, e] = total
            return total

        lax.fori_loop(0, NX * NC * CAP, entry, jnp.zeros((HALF, TW), jnp.float32), unroll=8)

    def drain_x(h):
        for d in range(1, NX):
            for cc in range(NC):
                send_x(h, d, cc).wait_send()
        send_own(h).wait_send()

    def drain_z(h):
        send_end(h).wait_send()
        for way in range(2):
            for step in range(4):
                for half in range(2):
                    if step or half == way:
                        send_z(h, way, step, half).wait_send()

    def turn(i, _):
        @pl.when(i < 2)
        def _():
            lax.fori_loop(0, TERMS // 2, lambda g, j: one(i * (TERMS // 2) + g, j), 1, unroll=4)

        @pl.when(i + 2 < STEPS)
        def _():
            start_x(i + 2)

        @pl.when(i < STEPS)
        def _():
            collect(i)
            z_step(i, 0, True)
            z_step(i, 1, False)

        for step in range(1, 4):
            @pl.when((i >= step) & (i - step < STEPS))
            def _(step=step):
                z_step(i - step, step, True)
                if step < 3:
                    z_step(i - step, step + 1, False)

        @pl.when((i >= 1) & (i < 5))
        def _():
            @pl.when(i == 1)
            def _():
                loads[5].wait()

            lax.fori_loop(i * 2 - 2, i * 2, cycle, 0)

            @pl.when(i == 4)
            def _():
                for d in range(1, 4):
                    send_y(d).start()

        @pl.when((i >= 2) & (i - 2 < STEPS))
        def _():
            drain_x(i - 2)

        @pl.when(i >= 5)
        def _():
            drain_z(i - 5)

        @pl.when(i >= 4)
        def _():
            finish(i - 4)

        return 0

    lax.fori_loop(0, STEPS + 4, turn, 0)

    def ending(h, _):
        send_end(h).wait_recv()
        rows = pl.ds((1 - core) * (TW // 2) + (h % QUARTERS) * HALF, HALF)
        for s in range(SLOTS):
            out_ref[h // QUARTERS, s, rows] = frecv[h, s]
        return 0

    lax.fori_loop(0, STEPS, ending, 0)

    loads[6].wait()
    for d in range(1, 4):
        send_y(d).wait_recv()

    def add(s, _):
        for j in range(J):
            total = out_ref[j, s] + exch_ref[j, s].astype(jnp.float32)
            total = total + ysend[y * J + j, s].astype(jnp.float32)
            for d in range(1, 4):
                total = total + yrecv[d, j, s].astype(jnp.float32)
            out_ref[j, s] = total
        return 0

    lax.fori_loop(0, SLOTS, add, 0)

    flags = flags_in[z]
    for d in range(1, NZ):
        source = (z + d) % NZ
        pltpu.make_async_copy(flags_in.at[source], flags_in.at[source], gr_sem.at[source]).wait()
        flags = flags + flags_in[source]
    pack_v[...] = jnp.broadcast_to(jnp.max(flags, axis=1, keepdims=True), (8, LANES))
    flag_copy = pltpu.make_async_copy(pack_v, flag_s, sm_sem.at[2])
    flag_copy.start()

    for d in range(1, NX * NC):
        send_label(d).wait_send()
    for d in range(1, NZ):
        send_flag(d).wait_send()
    for d in range(1, 4):
        send_y(d).wait_send()

    drain_z(STEPS - 1)
    flag_copy.wait()
    flag_ref[0] = flag_s[0, 0]


def main_call(sources, factors, blocks, owners, slots, amplitudes, exchange, left, right, ints):
    smem = pl.BlockSpec(memory_space=pltpu.SMEM)
    vmem = pl.BlockSpec(memory_space=pltpu.VMEM)
    hbm = pl.BlockSpec(memory_space=pl.ANY)
    dma = pltpu.SemaphoreType.DMA
    entries = NX * NC * CAP
    block = (J, SLOTS, TW, TW)
    return pl.pallas_call(
        main_kernel,
        out_shape=[
            jax.ShapeDtypeStruct(block, jnp.float32),
            jax.ShapeDtypeStruct((1,), jnp.int32),
        ],
        in_specs=[smem, vmem, vmem] + [hbm] * 7,
        out_specs=[vmem, smem],
        scratch_shapes=[
            pltpu.SMEM((8, TERMS), jnp.int32),
            pltpu.SMEM((8, TERMS), jnp.int32),
            pltpu.VMEM((8, LANES), jnp.int32),
            pltpu.VMEM(block, jnp.bfloat16),
            pltpu.VMEM(block, jnp.bfloat16),
            pltpu.VMEM((16, TW, TW), jnp.bfloat16),
            pltpu.VMEM((16, TW, TW), jnp.bfloat16),
            pltpu.VMEM((2, 2 * TW, 8 * TW), jnp.bfloat16),
            pltpu.VMEM((16, TW, TW), jnp.bfloat16),
            pltpu.VMEM((J, TERMS, TW, TW), jnp.bfloat16),
            pltpu.VMEM((STEPS, NX, NC, CAP, HALF, TW), jnp.bfloat16),
            pltpu.VMEM((STEPS, NX * NC, CAP, HALF, TW), jnp.bfloat16),
            pltpu.VMEM((entries, HALF, TW), jnp.bfloat16),
            pltpu.VMEM((STEPS, entries, HALF, TW), jnp.float32),
            pltpu.VMEM((STEPS, 2, 4, GOALS, HALF, TW), jnp.bfloat16),
            pltpu.VMEM((STEPS, 2, 4, GOALS, HALF, TW), jnp.bfloat16),
            pltpu.VMEM((8, SLOTS, TW, TW), jnp.bfloat16),
            pltpu.VMEM((4,) + block, jnp.bfloat16),
            pltpu.VMEM((STEPS, SLOTS, HALF, TW), jnp.float32),
            pltpu.VMEM((STEPS, SLOTS, HALF, TW), jnp.float32),
            pltpu.VMEM((NX, 8, LANES), jnp.int32),
            pltpu.VMEM((NX * NC, 8, LANES), jnp.int32),
            pltpu.VMEM((8, LANES), jnp.int32),
            pltpu.VMEM((NZ, 8, LANES), jnp.int32),
            pltpu.VMEM((8, LANES), jnp.int32),
            pltpu.VMEM((8, LANES), jnp.int32),
            pltpu.SMEM((8, LANES), jnp.int32),
            pltpu.SMEM((8, LANES), jnp.int32),
            pltpu.SMEM((8, LANES), jnp.int32),
            dma((7,)),
            dma((STEPS, NX, NC)),
            dma((STEPS,)),
            dma((STEPS, NX * NC)),
            dma((STEPS, 2, 4, 2)),
            dma((STEPS, 2, 4, 2)),
            dma((4,)),
            dma((4,)),
            dma((NX * NC,)),
            dma((NX * NC,)),
            dma((NZ,)),
            dma((NZ,)),
            dma((3,)),
            dma((STEPS,)),
            dma((STEPS,)),
        ],
        compiler_params=pltpu.CompilerParams(
            collective_id=0, has_side_effects=True, vmem_limit_bytes=58 * 2**20
        ),
        cost_estimate=pl.CostEstimate(
            flops=2 * 1024 * TW**3, bytes_accessed=8 * 2**20, transcendentals=0
        ),
    )(blocks, owners, slots, sources, factors, amplitudes, exchange, left, right, ints)


def spilled(
    amplitudes, left_factors, right_factors, ladder_sources, ladder_factors, keys
):
    tile = lax.axis_index("tile")
    table = lax.all_gather(keys, "tile", axis=0)
    column, rank = ranks_in_column(keys)
    packed = ladder_terms(
        ladder_sources, ladder_factors, column * TERMS + rank, amplitudes, left_factors,
        right_factors,
    ).reshape(J, NX, TERMS, TW, TW)
    width = TERMS - CAP
    all_ranks = ranks_in_column(table)[1]
    group = (tile // 8) * 8
    here = lax.dynamic_slice_in_dim(table, group, 8, 0).reshape(-1)
    here_rank = lax.dynamic_slice_in_dim(all_ranks, group, 8, 0).reshape(-1)
    number = jnp.arange(8 * TERMS, dtype=jnp.int32)
    valid = ((here // SLOTS) % 8 == tile % 8) & (here_rank >= CAP)
    target = jnp.where(valid, (here // (SLOTS * 8)) * SLOTS + here % SLOTS, 64)
    order = target * 256 + number
    place = jnp.sum((order[None, :] < order[:, None]).astype(jnp.int32), axis=1)
    hit = place[None, :] == number[:, None]
    spot = (number // TERMS) * width + jnp.maximum(here_rank - CAP, 0)
    perm = jnp.sum(jnp.where(hit, spot[None, :], 0), axis=1)
    sorted_target = jnp.sum(jnp.where(hit, target[None, :], 0), axis=1)
    same = jnp.concatenate(
        [jnp.zeros((1,), jnp.int32), (sorted_target[1:] == sorted_target[:-1]).astype(jnp.int32)]
    )
    goal = jnp.arange(64, dtype=jnp.int32)[:, None]
    end = jnp.maximum(jnp.sum((target[None, :] <= goal).astype(jnp.int32), axis=1) - 1, 0)
    some = jnp.sum((target[None, :] == goal).astype(jnp.int32), axis=1)
    entries = 8 * width
    return route(CAP, width, entries, 1, perm[:entries], same[:entries], end, some, packed)


def local(
    amplitudes, exchange_ints, left_factors, right_factors, ladder_sources, ladder_factors,
    dest_owners, dest_slots, cycle_blocks, cycle_ints,
):
    total, flags = main_call(
        ladder_sources.T, ladder_factors.T, cycle_blocks, dest_owners.reshape(1, TERMS),
        dest_slots[None, :], amplitudes, exchange_ints,
        left_factors, right_factors, cycle_ints,
    )

    def whole():
        return total.astype(jnp.bfloat16)

    def more():
        keys = dest_owners[:, 0] * SLOTS + dest_slots
        rest = spilled(
            amplitudes, left_factors, right_factors, ladder_sources, ladder_factors, keys
        )
        return (total + rest).astype(jnp.bfloat16)

    return lax.cond(flags[0] > 0, more, whole)


def solution(mesh):
    placed = (
        P("occ", "tile", None, None),
        P("occ", "tile", None, None),
        P("tile", None, None),
        P("tile", None, None),
        P("tile", None),
        P("tile", None),
        P("tile", None),
        P("tile"),
        P("tile"),
        P("tile", "occ", None),
    )
    return jax.shard_map(
        local, mesh=mesh, in_specs=placed, out_specs=P("occ", "tile", None, None), check_vma=False
    )
```
